32 devices in a mesh: sec: 4 (over y, x), lat: 8 (over z, core).
Axes of the slice: x: 2, y: 2, z: 4, core: 2. Of those that a mesh axis runs over, the one named last changes fastest.
Arguments:
- states: float32 [4, 3, 448, 4096], P('sec', None, 'lat'), may hold values from -40 to 40
- depth_field: float32 [448, 4096], P('lat'), may hold values from 0.07 to 1
- land_mask: int32 [448, 4096], P('lat'), may hold values 0 or 1
- tide_cos: float32 [448, 4096], P('lat'), may hold values from -8 to 8
- tide_sin: float32 [448, 4096], P('lat'), may hold values from -8 to 8
Outputs:
- new_states: float32 [4, 3, 448, 4096], P('sec', None, 'lat')
- mismatch: float32 [4, 3, 448, 4096], P('sec', None, 'lat')
- step_length: float32 [], replicated
The draws below stay inside these ranges and needn't reach their ends.
All inputs are finite; a program needn't handle non-finite values. No bound on the sum of `land_mask` on one device may be relied on, other than what follows from the above.
Results may differ from the reference program's by a relative error of at most 0.00002.
Values sent between devices are 32-bit elements; how exact they have to be, the bound alone decides.
A program may use at most 64 MiB of HBM per device.

```python
import math
import jax
import jax.numpy as jnp

LON = 4096
STEPS = 4
SECTIONS = 4
LATS = 448


def draw_states(key, part):
    key_base, key_rough = jax.random.split(key, 2)
    shape_all = (SECTIONS, 3, LATS, LON)
    base_values = jax.random.normal(key_base, shape_all, jnp.float32)
    rough_factor = jnp.exp(jax.random.uniform(key_rough, shape_all, jnp.float32, -0.7, 0.7))
    lat_ramp = 1.0 + 2.0 * jnp.arange(LATS, dtype=jnp.float32) / max(LATS - 1, 1)
    sec_ramp = 1.0 + jnp.arange(SECTIONS, dtype=jnp.float32) / max(SECTIONS - 1, 1)
    return 0.4 * base_values * rough_factor * lat_ramp[None, None, :, None] * sec_ramp[:, None, None, None]


def block_levels(key, row_low, row_high, col_low, col_high):
    key_row, key_col = jax.random.split(key, 2)
    row_levels = jax.random.uniform(key_row, (LATS // 8 + 1,), jnp.float32, row_low, row_high)
    col_levels = jax.random.uniform(key_col, (8,), jnp.float32, col_low, col_high)
    row_block = jnp.arange(LATS, dtype=jnp.int32) // 8
    col_block = jnp.arange(LON, dtype=jnp.int32) * 8 // LON
    return row_levels[row_block][:, None] + col_levels[col_block][None, :]


def draw_depth_field(key, part):
    key_level, key_cell = jax.random.split(jax.random.fold_in(key, 11), 2)
    levels = block_levels(key_level, -1.2, 0.0, -0.6, 0.0)
    cell_levels = jax.random.uniform(key_cell, (LATS, LON), jnp.float32, -0.35, 0.0)
    return jnp.exp(levels + cell_levels)


def tide_draw(key, constant):
    key_level, key_value = jax.random.split(jax.random.fold_in(key, constant), 2)
    levels = block_levels(key_level, -0.8, 0.8, -0.4, 0.4)
    values = jnp.clip(jax.random.normal(key_value, (LATS, LON), jnp.float32), -4.0, 4.0)
    return jnp.clip(values * jnp.exp(levels), -8.0, 8.0)


def draw_tide_cos(key, part):
    return tide_draw(key, 23)


def draw_tide_sin(key, part):
    return tide_draw(key, 37)


def plant(entries, stream_key, low, top_value):
    longest = entries.shape.index(max(entries.shape))
    spots = []
    for shift in (0, 1):
        where = [jax.random.randint(jax.random.fold_in(stream_key, axis), (), 0, length) for axis, length in enumerate(entries.shape)]
        where[longest] = (where[longest] + shift) % entries.shape[longest]
        spots.append(tuple(where))
    return entries.at[spots[0]].set(low).at[spots[1]].set(top_value)


def setup_inputs(seed: int = 0) -> dict:
    key_of = jax.random.split(jax.random.key(seed), 6)
    return {
        "states": draw_states(jax.random.fold_in(key_of[5], 71), 0),
        "depth_field": draw_depth_field(jax.random.fold_in(key_of[5], 71), 0),
        "land_mask": plant((jax.random.randint(key_of[2], (LATS, LON), 0, 10) < 7).astype(jnp.int32), jax.random.fold_in(key_of[2], 1), 0, 1),
        "tide_cos": draw_tide_cos(jax.random.fold_in(key_of[5], 71), 0),
        "tide_sin": draw_tide_sin(jax.random.fold_in(key_of[5], 71), 0),
    }


DRAG_RATE = 0.9
CORIOLIS_MAX = 0.3
PUSH_RATE = 1.0
FLOW_RATE = 1.0
EPSILON = 1e-6
TWO_PI = 2.0 * math.pi


def along_lon(source):
    return 0.5 * (jnp.roll(source, -1, axis=-1) - jnp.roll(source, 1, axis=-1))


def along_lat(source):
    widths = [(0, 0)] * (source.ndim - 2) + [(1, 1), (0, 0)]
    padded = jnp.pad(source, widths)
    return 0.5 * (padded[..., 2:, :] - padded[..., :-2, :])


def forward_step(height, east_flow, north_flow, wet_field, sea_field, coriolis, forcing):
    raised = height + forcing
    east_new = sea_field * (DRAG_RATE * east_flow + coriolis * north_flow - PUSH_RATE * along_lon(raised))
    north_new = sea_field * (DRAG_RATE * north_flow - coriolis * east_flow - PUSH_RATE * along_lat(raised))
    height_new = height - FLOW_RATE * along_lon(wet_field * east_new) - FLOW_RATE * along_lat(wet_field * north_new)
    return height_new, east_new, north_new


def adjoint_step(height_cot, east_cot, north_cot, wet_field, sea_field, coriolis):
    east_mid = sea_field * (east_cot + FLOW_RATE * wet_field * along_lon(height_cot))
    north_mid = sea_field * (north_cot + FLOW_RATE * wet_field * along_lat(height_cot))
    height_new = height_cot + PUSH_RATE * along_lon(east_mid) + PUSH_RATE * along_lat(north_mid)
    east_new = DRAG_RATE * east_mid - coriolis * north_mid
    north_new = coriolis * east_mid + DRAG_RATE * north_mid
    return height_new, east_new, north_new


def reference(states, depth_field, land_mask, tide_cos, tide_sin):
    sea_field = land_mask.astype(jnp.float32)
    wet_field = depth_field * sea_field
    row_values = jnp.arange(LATS, dtype=jnp.int32).astype(jnp.float32)
    coriolis = (CORIOLIS_MAX * jnp.sin(jnp.pi * (row_values + 0.5) / LATS - 0.5 * jnp.pi))[:, None]

    def integrate(fields, forced):
        height, east_flow, north_flow = fields[:, 0], fields[:, 1], fields[:, 2]
        for segment_index in range(STEPS):
            if forced:
                phase_angle = TWO_PI * (jnp.arange(SECTIONS, dtype=jnp.int32) * STEPS + segment_index).astype(jnp.float32) / (SECTIONS * STEPS)
                forcing = jnp.cos(phase_angle)[:, None, None] * tide_cos + jnp.sin(phase_angle)[:, None, None] * tide_sin
            else:
                forcing = jnp.zeros((), jnp.float32)
            height, east_flow, north_flow = forward_step(height, east_flow, north_flow, wet_field, sea_field, coriolis, forcing)
        return jnp.stack([height, east_flow, north_flow], axis=1)

    ending = integrate(states, True)
    mismatch = ending - jnp.roll(states, -1, axis=0)
    height, east_flow, north_flow = mismatch[:, 0], mismatch[:, 1], mismatch[:, 2]
    for segment_index in range(STEPS):
        height, east_flow, north_flow = adjoint_step(height, east_flow, north_flow, wet_field, sea_field, coriolis)
    adjoint = jnp.stack([height, east_flow, north_flow], axis=1)
    gradient = adjoint - jnp.roll(mismatch, 1, axis=0)
    image = integrate(gradient, False) - jnp.roll(gradient, -1, axis=0)
    total_count = SECTIONS * 3 * LATS * LON
    grad_mean = jnp.sum(gradient * gradient) / total_count
    image_mean = jnp.sum(image * image) / total_count
    step_length = grad_mean / (image_mean + EPSILON)
    new_states = states - step_length * gradient
    return new_states, mismatch, step_length
```

```python
import functools
import math

import jax
import jax.numpy as jnp
import numpy as np
from jax import lax
from jax.experimental import pallas as pl
from jax.experimental.pallas import tpu as pltpu
from jax.sharding import PartitionSpec as P

STEPS = 4
DRAG_RATE = 0.9
CORIOLIS_MAX = 0.3
EPSILON = 1e-06
TWO_PI = 2.0 * math.pi
HALO = 24
MESH = pl.DeviceIdType.MESH


def kernel(
    sections, bands, count,
    states, depth, mask, tide_one, tide_two, rows_in, trig,
    home, full, step_out,
    wide, raw, mask_win, fold, unfold, stage, mis_out, grad_out, st, start, mis, grad,
    high, east, north, raised, flux, fluy, acc, part, total,
    load_sem, s1, r1, halo_s, halo_r, st_s, st_r, s2, r2, s3, r3, own_sem, ps, pr, ts, tr,
):
    me = lax.axis_index("sec")
    band = lax.axis_index("lat")
    rows, lon = states.shape[1], states.shape[2]
    share = lon // sections
    per, tiles = share // 128, lon // 128
    wins = per + 1
    group = 3 if wins % 3 == 0 else wins
    groups = wins // group
    block = wide.shape[2]
    tall = rows + 2 * HALO
    strips = tall // 8
    top, low = HALO, HALO + rows

    def peer(i):
        return lax.rem(me + i, sections)

    def tile(c):
        return pl.ds(pl.multiple_of(c * 128, 128), 128)

    def load_states(c, _):
        src = states.at[:, :, tile(c)]
        dst = wide.at[c + c // per, :, pl.ds(0, rows), :]
        pltpu.make_async_copy(src, dst, load_sem.at[0]).start()
        return 0

    lax.fori_loop(0, tiles, load_states, 0)
    singles = (
        (depth, raw.at[:, 0, pl.ds(0, rows)]),
        (mask, mask_win),
        (tide_one, raw.at[:, 2, pl.ds(0, rows)]),
        (tide_two, raw.at[:, 3, pl.ds(0, rows)]),
    )

    def load_static(c, _):
        ahead = jnp.where(c == wins, tiles - 1, c)
        at = tile(lax.rem(me * per + ahead, tiles))
        for n, (src, dst) in enumerate(singles):
            pltpu.make_async_copy(src.at[:, at], dst.at[c], load_sem.at[1 + n]).start()
        return 0

    lax.fori_loop(0, wins + 1, load_static, 0)

    span = 128 * group

    def build(r, _):
        at = pl.ds(pl.multiple_of(16 * r, 16), 16)
        row = lax.broadcasted_iota(jnp.int32, (16, 128), 0) + 16 * r
        lane = lax.broadcasted_iota(jnp.int32, (16, 128), 1)
        for c in range(group):
            cols = slice(c * 128, c * 128 + 128)
            fold[at, cols] = jnp.where(row == group * lane + c, 1.0, 0.0).astype(jnp.bfloat16)
            source = group * (row % 128) + row // 128
            unfold[at, cols] = jnp.where(source == lane + c * 128, 1.0, 0.0).astype(jnp.bfloat16)
        return 0

    lax.fori_loop(0, span // 16, build, 0)

    def permute(matrix, fields, load, store):
        high_part = fields * block

        def one(g, _):
            def split(i, _):
                a, r = i // (block // 16), lax.rem(i, block // 16)
                to = pl.ds(pl.multiple_of(16 * i, 16), 16)
                for c in range(group):
                    x = load(g * group + c, a, 16 * r)
                    high = x.astype(jnp.bfloat16)
                    rest = x - high.astype(jnp.float32)
                    middle = rest.astype(jnp.bfloat16)
                    last = (rest - middle.astype(jnp.float32)).astype(jnp.bfloat16)
                    cols = slice(c * 128, c * 128 + 128)
                    stage[0, to, cols] = high
                    stage[1, to, cols] = middle
                    stage[2, to, cols] = last
                return 0

            lax.fori_loop(0, high_part // 16, split, 0)
            lhs = stage[:, :high_part, :].reshape(3 * high_part, span)
            y = jnp.dot(lhs, matrix[...], preferred_element_type=jnp.float32)
            z = y[:high_part] + y[high_part : 2 * high_part] + y[2 * high_part :]
            for c in range(group):
                for a in range(fields):
                    store(g, c, a, z[a * block : a * block + rows, c * 128 : c * 128 + 128])
            return 0

        lax.fori_loop(0, groups, one, 0)

    barrier = pltpu.get_barrier_semaphore()
    for i in range(1, sections):
        pl.semaphore_signal(barrier, inc=1, device_id={"sec": peer(i)}, device_id_type=MESH)
    for i in range(1, bands):
        pl.semaphore_signal(
            barrier, inc=1, device_id={"lat": lax.rem(band + i, bands)}, device_id_type=MESH
        )
    pl.semaphore_wait(barrier, sections + bands - 2)

    loaded = wide.at[pl.ds(0, tiles), :, pl.ds(0, rows), :]
    pltpu.make_async_copy(loaded, loaded, load_sem.at[0]).wait()
    early = lax.broadcasted_iota(jnp.int32, (8, 128), 1) < 64

    def pack(r, _):
        at = pl.ds(pl.multiple_of(8 * r, 8), 8)
        for j in range(sections):
            after, before = (j + 1) % sections * wins, (j - 1) % sections * wins + per - 1
            for a in range(3):
                wide[j * wins + per, a, at, :] = jnp.where(
                    early, wide[after, a, at, :], wide[before, a, at, :]
                )
        return 0

    lax.fori_loop(0, rows // 8, pack, 0)

    def piece(j, slot):
        return pltpu.make_async_remote_copy(
            src_ref=wide.at[pl.ds(j * wins, wins), :, pl.ds(0, rows), :],
            dst_ref=start.at[me, :, :, pl.ds(top, rows), :],
            send_sem=s1.at[j],
            recv_sem=r1.at[slot],
            device_id={"sec": j},
            device_id_type=MESH,
        )

    def turn(n):
        return lax.rem(me + jnp.where(lax.rem(me, 2) == 0, n, sections - n), sections)

    def fold_piece(j):
        def load(w, a, r):
            return wide[j * wins + w, a, pl.ds(pl.multiple_of(r, 16), 16), :]

        def store(g, c, a, x):
            wide[j * wins + g * group + c, a, pl.ds(0, rows), :] = x

        permute(fold, 3, load, store)

    def launch(n, _):
        fold_piece(turn(n))
        piece(turn(n), me).start()
        return 0

    lax.fori_loop(1, sections - 1, launch, 0)
    fold_piece(me)
    own = pltpu.make_async_copy(
        wide.at[pl.ds(me * wins, wins), :, pl.ds(0, rows), :],
        start.at[me, :, :, pl.ds(top, rows), :],
        own_sem.at[0],
    )
    own.start()

    up_ok, down_ok = band > 0, band < bands - 1

    def to_above(s):
        return pltpu.make_async_remote_copy(
            src_ref=start.at[s, :, :, pl.ds(top, HALO), :],
            dst_ref=start.at[s, :, :, pl.ds(low, HALO), :],
            send_sem=halo_s.at[0, s], recv_sem=halo_r.at[0, s],
            device_id={"lat": band - 1}, device_id_type=MESH,
        )

    def to_below(s):
        return pltpu.make_async_remote_copy(
            src_ref=start.at[s, :, :, pl.ds(low - HALO, HALO), :],
            dst_ref=start.at[s, :, :, pl.ds(0, HALO), :],
            send_sem=halo_s.at[1, s], recv_sem=halo_r.at[1, s],
            device_id={"lat": band + 1}, device_id_type=MESH,
        )

    def st_above():
        return pltpu.make_async_remote_copy(
            src_ref=st.at[:, :, pl.ds(top, HALO), :], dst_ref=st.at[:, :, pl.ds(low, HALO), :],
            send_sem=st_s.at[0], recv_sem=st_r.at[0],
            device_id={"lat": band - 1}, device_id_type=MESH,
        )

    def st_below():
        return pltpu.make_async_remote_copy(
            src_ref=st.at[:, :, pl.ds(low - HALO, HALO), :], dst_ref=st.at[:, :, pl.ds(0, HALO), :],
            send_sem=st_s.at[1], recv_sem=st_r.at[1],
            device_id={"lat": band + 1}, device_id_type=MESH,
        )

    def send_halo(s):
        @pl.when(up_ok)
        def _():
            to_above(s).start()

        @pl.when(down_ok)
        def _():
            to_below(s).start()

    def recv_halo(s):
        @pl.when(down_ok)
        def _():
            to_above(s).wait_recv()

        @pl.when(up_ok)
        def _():
            to_below(s).wait_recv()

    own.wait()
    send_halo(me)

    for n, (src, dst) in enumerate(singles):
        pltpu.make_async_copy(dst, dst, load_sem.at[1 + n]).wait()

    def prepare(r, _):
        at = pl.ds(pl.multiple_of(8 * r, 8), 8)
        for c in range(wins + 1):
            sea = mask_win[c, at, :].astype(jnp.float32)
            raw[c, 1, at, :] = sea
            raw[c, 0, at, :] = raw[c, 0, at, :] * sea
        for a in range(4):
            raw[per, a, at, :] = jnp.where(early, raw[per, a, at, :], raw[wins, a, at, :])
        return 0

    lax.fori_loop(0, rows // 8, prepare, 0)

    def load_raw(w, a, r):
        return raw[w, a, pl.ds(pl.multiple_of(r, 16), 16), :]

    def store_st(g, c, a, x):
        st[a, g * group + c, pl.ds(top, rows), :] = x

    permute(fold, 4, load_raw, store_st)

    @pl.when(up_ok)
    def _():
        st_above().start()

    @pl.when(down_ok)
    def _():
        st_below().start()

    zero = jnp.zeros((8, 128), jnp.float32)

    def blank(first):
        def body(r, _):
            at = pl.ds(pl.multiple_of(first + 8 * r, 8), 8)
            for c in range(wins):
                for a in range(4):
                    st[a, c, at, :] = zero
                for s in range(sections):
                    for a in range(3):
                        start[s, c, a, at, :] = zero
            return 0

        lax.fori_loop(0, HALO // 8, body, 0)

    @pl.when(band == 0)
    def _():
        blank(0)

    @pl.when(band == bands - 1)
    def _():
        blank(low)

    def edge(lo, hi):
        for buf in (raised, flux):
            for c in range(wins):
                buf[c, pl.ds(8 * lo, 8), :] = zero
                buf[c, pl.ds(8 * hi + 8, 8), :] = zero

    acc[...] = jnp.zeros_like(acc)

    @pl.when(down_ok)
    def _():
        st_above().wait_recv()

    @pl.when(up_ok)
    def _():
        st_below().wait_recv()

    lane = lax.broadcasted_iota(jnp.int32, (8, 128), 1)

    def lon_diff(xs, w):
        g, c = w // group, w % group
        first, last = g * group, g * group + group - 1
        if c < group - 1:
            after = xs[w + 1]
        else:
            after = xs[first]
            if groups > 1:
                after = jnp.where(lane == 0, xs[(w + 1) % wins], after)
            after = pltpu.roll(after, 127, 1)
        if c > 0:
            before = xs[w - 1]
        else:
            before = xs[last]
            if groups > 1:
                before = jnp.where(lane == 127, xs[w - 1], before)
            before = pltpu.roll(before, 1, 1)
        return after - before

    def owned(w):
        g, c = w // group, w % group
        return max(0, min(128, -((g * span + c - share) // group)))

    def own_sum(xs):
        total_own = None
        for w, x in enumerate(xs):
            n = owned(w)
            if n == 0:
                continue
            x = x if n == 128 else jnp.where(lane < n, x, 0.0)
            total_own = x if total_own is None else total_own + x
        return total_own

    def lat_diff(ref, c, r0):
        return ref[c, pl.ds(r0 + 9, 8), :] - ref[c, pl.ds(r0 + 7, 8), :]

    def run(kind, source, s, lo, hi, finish, target_of=None):
        def push(h, c, at, step):
            if kind != "forced":
                return 0.5 * h
            base = 2 * (s * STEPS + step)
            return 0.5 * (h + (trig[base] * st[2, c, at, :] + trig[base + 1] * st[3, c, at, :]))

        def begin(r, _):
            r0 = pl.multiple_of(8 * r, 8)
            at = pl.ds(r0, 8)
            for c in range(wins):
                raised[c, pl.ds(pl.multiple_of(r0 + 8, 8), 8), :] = push(
                    source[s, c, 0, at, :], c, at, 0
                )
            return 0

        lax.fori_loop(lo, hi, begin, 0)
        edge(lo, hi)
        for step in range(STEPS):
            def first(r, _):
                r0 = pl.multiple_of(8 * r, 8)
                at = pl.ds(r0, 8)
                padded = pl.ds(pl.multiple_of(r0 + 8, 8), 8)
                cor = rows_in[0, at, :]
                xs = [raised[c, padded, :] for c in range(wins)]
                out = []
                for c in range(wins):
                    wet, sea = st[0, c, at, :], st[1, c, at, :]
                    dx, dy = lon_diff(xs, c), lat_diff(raised, c, r0)
                    if step == 0:
                        u, v = source[s, c, 1, at, :], source[s, c, 2, at, :]
                    else:
                        u, v = east[c, at, :], north[c, at, :]
                    if kind == "back":
                        e = sea * (u + wet * dx)
                        f = sea * (v + wet * dy)
                        out.append((
                            DRAG_RATE * e - cor * f, cor * e + DRAG_RATE * f, 0.5 * e, 0.5 * f
                        ))
                    else:
                        e = sea * (DRAG_RATE * u + cor * v - dx)
                        f = sea * (DRAG_RATE * v - cor * u - dy)
                        half = 0.5 * wet
                        out.append((e, f, half * e, half * f))
                for c in range(wins):
                    east[c, at, :], north[c, at, :] = out[c][0], out[c][1]
                    fluy[c, at, :], flux[c, padded, :] = out[c][2], out[c][3]
                return 0

            lax.fori_loop(lo, hi, first, 0)

            def second(r, _):
                r0 = pl.multiple_of(8 * r, 8)
                at = pl.ds(r0, 8)
                inside = rows_in[1, at, :]
                xs = [fluy[c, at, :] for c in range(wins)]
                out = []
                for c in range(wins):
                    d = lon_diff(xs, c) + lat_diff(flux, c, r0)
                    h = source[s, c, 0, at, :] if step == 0 else high[c, at, :]
                    h = (h + d if kind == "back" else h - d) * inside
                    if step == STEPS - 1:
                        out.append(finish(c, at, (h, east[c, at, :], north[c, at, :])))
                    else:
                        out.append((h, push(h, c, at, step + 1)))
                if step < STEPS - 1:
                    ahead = pl.ds(pl.multiple_of(r0 + 8, 8), 8)
                    for c in range(wins):
                        high[c, at, :], raised[c, ahead, :] = out[c]
                elif kind == "free":
                    acc[0] += own_sum([x for x, _ in out])
                    acc[1] += own_sum([x for _, x in out])
                else:
                    target, slot = target_of
                    for c in range(wins):
                        for a in range(3):
                            target[slot, c, a, at, :] = out[c][a]
                return 0

            inner = 1 if step == STEPS - 1 else 0
            lax.fori_loop(lo + inner, hi - inner, second, 0)

    recv_halo(me)

    def keep(c, at, values):
        return values

    run("forced", start, me, 0, strips, keep, (mis, me))

    for n in range(1, sections - 1):
        piece(turn(n), me).wait_send()
    fold_piece(turn(sections - 1))
    piece(turn(sections - 1), me).start()

    def arrive(n):
        s = turn(n)
        piece(s, s).wait_recv()
        send_halo(s)

    for n in range(1, sections - 1):
        arrive(n)

    def forced(n, _):
        @pl.when(n == sections - 2)
        def _():
            arrive(sections - 1)

        s = turn(n)
        recv_halo(s)
        run("forced", start, s, 0, strips, keep, (mis, s))
        return 0

    lax.fori_loop(1, sections, forced, 0)

    def subtract(s, after):
        def body(r, _):
            at = pl.ds(pl.multiple_of(8 * r, 8), 8)
            out = [
                [mis[s, c, a, at, :] - start[after, c, a, at, :] for a in range(3)]
                for c in range(wins)
            ]
            for c in range(wins):
                for a in range(3):
                    mis[s, c, a, at, :] = out[c][a]
            return 0

        lax.fori_loop(1, strips - 1, body, 0)

    def unfold_piece(source, target, s):
        def load(w, a, r):
            return source[s, w, a, pl.ds(pl.multiple_of(top + r, 8), 16), :]

        def store(g, c, a, x):
            @pl.when(g * group + c < per)
            def _():
                target[s, g * group + c, a] = x

        permute(unfold, 3, load, store)

    subtract(me, peer(1))
    unfold_piece(mis, mis_out, me)
    columns = pl.ds(me * per, per)
    own_mis = pltpu.make_async_copy(
        mis_out.at[me],
        home.at[columns],
        own_sem.at[1],
    )
    own_mis.start()

    def give(source, target, send, recv, s, at_columns, slot):
        return pltpu.make_async_remote_copy(
            src_ref=source.at[s],
            dst_ref=target.at[at_columns],
            send_sem=send.at[s], recv_sem=recv.at[slot],
            device_id={"sec": s}, device_id_type=MESH,
        )

    def differ(i, _):
        s = peer(i)
        subtract(s, peer(i + 1))
        unfold_piece(mis, mis_out, s)
        give(mis_out, home, s2, r2, s, columns, me).start()
        return 0

    lax.fori_loop(1, sections, differ, 0)

    def back(i, _):
        s = peer(i)
        before = peer(i + sections - 1)

        def done(c, at, values):
            return [x - mis[before, c, a, at, :] for a, x in enumerate(values)]

        run("back", mis, s, 1, strips - 1, done, (grad, s))

        unfold_piece(grad, grad_out, s)

        @pl.when(i < sections)
        def _():
            give(grad_out, full, s3, r3, s, columns, me).start()

        return 0

    lax.fori_loop(1, sections + 1, back, 0)
    own_grad = pltpu.make_async_copy(
        grad_out.at[me],
        full.at[columns],
        own_sem.at[2],
    )
    own_grad.start()

    def image(i, _):
        s = peer(i)
        after = peer(i + 1)

        def squares(c, at, values):
            pairs = [(x, grad[after, c, a, at, :]) for a, x in enumerate(values)]
            return sum(g * g for _, g in pairs), sum((x - g) * (x - g) for x, g in pairs)

        run("free", grad, s, 2, strips - 2, squares)
        return 0

    lax.fori_loop(0, sections, image, 0)

    part[me] = acc[...]

    def share_part(j, slot):
        return pltpu.make_async_remote_copy(
            src_ref=acc, dst_ref=part.at[slot], send_sem=ps.at[j], recv_sem=pr.at[slot],
            device_id={"sec": j}, device_id_type=MESH,
        )

    for i in range(1, sections):
        share_part(peer(i), me).start()
    for i in range(1, sections):
        share_part(peer(i), peer(i)).wait_recv()
    for i in range(1, sections):
        share_part(peer(i), me).wait_send()
    summed = part[0]
    for s in range(1, sections):
        summed = summed + part[s]
    acc[...] = summed
    total[band] = summed

    def share_total(j, slot):
        return pltpu.make_async_remote_copy(
            src_ref=acc, dst_ref=total.at[slot], send_sem=ts.at[j], recv_sem=tr.at[slot],
            device_id={"lat": j}, device_id_type=MESH,
        )

    for i in range(1, bands):
        share_total(lax.rem(band + i, bands), band).start()
    for i in range(1, bands):
        j = lax.rem(band + i, bands)
        share_total(j, j).wait_recv()
    summed = total[0]
    for s in range(1, bands):
        summed = summed + total[s]
    sums = jnp.sum(jnp.sum(summed, axis=2, keepdims=True), axis=1, keepdims=True)
    step = sums[0] / count / (sums[1] / count + EPSILON)
    step_out[...] = jnp.broadcast_to(step, (8, 128))

    own_mis.wait()

    def mismatches(i, _):
        s = peer(i)
        give(mis_out, home, s2, r2, s, columns, s).wait()
        return 0

    lax.fori_loop(1, sections, mismatches, 0)

    own_grad.wait()

    def grads(i, _):
        s = peer(i)
        give(grad_out, full, s3, r3, s, columns, s).wait_recv()
        return 0

    lax.fori_loop(1, sections, grads, 0)


    piece(turn(sections - 1), me).wait_send()

    def drain(i, _):
        s = peer(i)
        give(grad_out, full, s3, r3, s, columns, me).wait_send()
        return 0

    lax.fori_loop(1, sections, drain, 0)

    def drain_halo(i, _):
        s = peer(i)

        @pl.when(up_ok)
        def _():
            to_above(s).wait_send()

        @pl.when(down_ok)
        def _():
            to_below(s).wait_send()

        return 0

    lax.fori_loop(0, sections, drain_halo, 0)

    @pl.when(up_ok)
    def _():
        st_above().wait_send()

    @pl.when(down_ok)
    def _():
        st_below().wait_send()

    for i in range(1, bands):
        share_total(lax.rem(band + i, bands), band).wait_send()


def finish_kernel(fields, home, full, step, new_fields, mismatch):
    rows, share = fields.shape[1:]
    length = step[0:1, :]

    def body(r, _):
        at = pl.ds(pl.multiple_of(8 * r, 8), 8)
        for c in range(share // 128):
            cols = slice(c * 128, c * 128 + 128)
            for a in range(3):
                new_fields[a, at, cols] = fields[a, at, cols] - length * full[c, a, at, :]
                mismatch[a, at, cols] = home[c, a, at, :]
        return 0

    lax.fori_loop(0, rows // 8, body, 0)


def shards(states, depth_field, land_mask, tide_cos, tide_sin):
    fields = states[0]
    rows, lon = fields.shape[1:]
    sections, bands = lax.axis_size("sec"), lax.axis_size("lat")
    band = lax.axis_index("lat")
    share = lon // sections
    tall = rows + 2 * HALO
    lat_total = rows * bands
    ids = band * rows - HALO + jnp.arange(tall, dtype=jnp.int32)
    inside = ((ids >= 0) & (ids < lat_total)).astype(jnp.float32)
    coriolis = CORIOLIS_MAX * jnp.sin(
        jnp.pi * (ids.astype(jnp.float32) + 0.5) / lat_total - 0.5 * jnp.pi
    )
    rows_in = jnp.broadcast_to(jnp.stack([coriolis, inside])[:, :, None], (2, tall, 128))
    angles = np.float32(TWO_PI) * np.arange(sections * STEPS, dtype=np.float32) / np.float32(
        sections * STEPS
    )
    trig = jnp.asarray(np.stack([np.cos(angles), np.sin(angles)], axis=1).reshape(-1))
    f32 = jnp.float32
    dma = pltpu.SemaphoreType.DMA
    any_spec = pl.BlockSpec(memory_space=pl.ANY)
    vmem = pl.BlockSpec(memory_space=pltpu.VMEM)
    tiles, wins = lon // 128, share // 128 + 1
    stacked = pltpu.VMEM((sections, wins, 3, tall, 128), f32)
    plain = pltpu.VMEM((wins, tall, 128), f32)
    padded = pltpu.VMEM((wins, tall + 16, 128), f32)
    block = -(-rows // 16) * 16
    span = 128 * (3 if wins % 3 == 0 else wins)
    returned = pltpu.VMEM((sections, wins - 1, 3, rows, 128), f32)
    gathered = jax.ShapeDtypeStruct((tiles, 3, rows, 128), f32)
    home, full, step = pl.pallas_call(
        functools.partial(kernel, sections, bands, float(sections * 3 * lat_total * lon)),
        out_shape=(
            gathered,
            gathered,
            jax.ShapeDtypeStruct((8, 128), f32),
        ),
        in_specs=[any_spec] * 5 + [vmem, pl.BlockSpec(memory_space=pltpu.SMEM)],
        out_specs=(any_spec, any_spec, vmem),
        scratch_shapes=[
            pltpu.VMEM((tiles + sections, 3, block, 128), f32),
            pltpu.VMEM((wins + 1, 4, block, 128), f32),
            pltpu.VMEM((wins + 1, rows, 128), jnp.int32),
            pltpu.VMEM((span, span), jnp.bfloat16),
            pltpu.VMEM((span, span), jnp.bfloat16),
            pltpu.VMEM((3, 4 * block, span), jnp.bfloat16),
            returned, returned,
            pltpu.VMEM((4, wins, tall, 128), f32),
            stacked, stacked, stacked,
            plain, plain, plain, padded, padded, plain,
            pltpu.VMEM((2, 8, 128), f32),
            pltpu.VMEM((sections, 2, 8, 128), f32),
            pltpu.VMEM((bands, 2, 8, 128), f32),
            dma((5,)),
            dma((sections,)), dma((sections,)),
            dma((2, sections)), dma((2, sections)),
            dma((2,)), dma((2,)),
            dma((sections,)), dma((sections,)),
            dma((sections,)), dma((sections,)),
            dma((3,)),
            dma((sections,)), dma((sections,)),
            dma((bands,)), dma((bands,)),
        ],
        compiler_params=pltpu.CompilerParams(
            collective_id=0, has_side_effects=True, vmem_limit_bytes=60 * 1024 * 1024
        ),
        name="shooting",
    )(fields, depth_field, land_mask, tide_cos, tide_sin, rows_in, trig)
    block = pl.BlockSpec((3, rows, share), lambda i: (0, 0, i))
    by_tile = pl.BlockSpec((share // 128, 3, rows, 128), lambda i: (i, 0, 0, 0))
    new_fields, mismatch = pl.pallas_call(
        finish_kernel,
        grid=(sections,),
        out_shape=(jax.ShapeDtypeStruct(fields.shape, f32),) * 2,
        in_specs=[block, by_tile, by_tile, pl.BlockSpec((8, 128), lambda i: (0, 0))],
        out_specs=(block, block),
        compiler_params=pltpu.CompilerParams(vmem_limit_bytes=32 * 1024 * 1024),
        name="update",
    )(fields, home, full, step)
    return new_fields[None], mismatch[None], step[0, 0]


def solution(mesh):
    return jax.shard_map(
        shards,
        mesh=mesh,
        in_specs=(
            P("sec", None, "lat", None),
            P("lat", None),
            P("lat", None),
            P("lat", None),
            P("lat", None),
        ),
        out_specs=(P("sec", None, "lat", None), P("sec", None, "lat", None), P()),
        check_vma=False,
    )
```

```python
import functools
import math

import jax
import jax.numpy as jnp
import numpy as np
from jax import lax
from jax.experimental import pallas as pl
from jax.experimental.pallas import tpu as pltpu
from jax.sharding import PartitionSpec as P

STEPS = 4
DRAG_RATE = 0.9
CORIOLIS_MAX = 0.3
EPSILON = 1e-06
TWO_PI = 2.0 * math.pi
HALO = 24
STRIPS = 7
MESH = pl.DeviceIdType.MESH


def kernel(
    sections, bands, count,
    states, depth, mask, tide_one, tide_two, rows_in, trig,
    home, full, step_out,
    wide, mask_win, st, start, mis, grad,
    high, east, north, raised, flux, fluy, acc, part, total,
    load_sem, s1, r1, halo_s, halo_r, st_s, st_r, s2, r2, s3, r3, own_sem, ps, pr, ts, tr,
):
    me = lax.axis_index("sec")
    band = lax.axis_index("lat")
    rows, lon = states.shape[1], states.shape[2]
    share = lon // sections
    per, tiles = share // 128, lon // 128
    wins = per + 1
    tall = rows + 2 * HALO
    strips = tall // 8
    top, low = HALO, HALO + rows

    def peer(i):
        return lax.rem(me + i, sections)

    def tile(c):
        return pl.ds(pl.multiple_of(c * 128, 128), 128)

    def load_states(c, _):
        src = states.at[:, :, tile(c)]
        pltpu.make_async_copy(src, wide.at[c + c // per], load_sem.at[0]).start()
        return 0

    lax.fori_loop(0, tiles, load_states, 0)
    singles = (
        (depth, st.at[0, :, pl.ds(top, rows)]),
        (mask, mask_win),
        (tide_one, st.at[2, :, pl.ds(top, rows)]),
        (tide_two, st.at[3, :, pl.ds(top, rows)]),
    )

    def load_static(c, _):
        ahead = jnp.where(c == wins, tiles - 1, c)
        at = tile(lax.rem(me * per + ahead, tiles))
        for n, (src, dst) in enumerate(singles):
            pltpu.make_async_copy(src.at[:, at], dst.at[c], load_sem.at[1 + n]).start()
        return 0

    lax.fori_loop(0, wins + 1, load_static, 0)

    barrier = pltpu.get_barrier_semaphore()
    for i in range(1, sections):
        pl.semaphore_signal(barrier, inc=1, device_id={"sec": peer(i)}, device_id_type=MESH)
    for i in range(1, bands):
        pl.semaphore_signal(
            barrier, inc=1, device_id={"lat": lax.rem(band + i, bands)}, device_id_type=MESH
        )
    pl.semaphore_wait(barrier, sections + bands - 2)

    loaded = wide.at[pl.ds(0, tiles)]
    pltpu.make_async_copy(loaded, loaded, load_sem.at[0]).wait()
    early = lax.broadcasted_iota(jnp.int32, (8, 128), 1) < 64

    def pack(r, _):
        at = pl.ds(pl.multiple_of(8 * r, 8), 8)
        for j in range(sections):
            after, before = (j + 1) % sections * wins, (j - 1) % sections * wins + per - 1
            for a in range(3):
                wide[j * wins + per, a, at, :] = jnp.where(
                    early, wide[after, a, at, :], wide[before, a, at, :]
                )
        return 0

    lax.fori_loop(0, rows // 8, pack, 0)

    def piece(j, slot):
        return pltpu.make_async_remote_copy(
            src_ref=wide.at[pl.ds(j * wins, wins)],
            dst_ref=start.at[me, :, :, pl.ds(top, rows), :],
            send_sem=s1.at[j],
            recv_sem=r1.at[slot],
            device_id={"sec": j},
            device_id_type=MESH,
        )

    def turn(n):
        return lax.rem(me + jnp.where(lax.rem(me, 2) == 0, n, sections - n), sections)

    for n in range(1, sections - 1):
        piece(turn(n), me).start()
    own = pltpu.make_async_copy(
        wide.at[pl.ds(me * wins, wins)],
        start.at[me, :, :, pl.ds(top, rows), :],
        own_sem.at[0],
    )
    own.start()

    up_ok, down_ok = band > 0, band < bands - 1

    def to_above(s):
        return pltpu.make_async_remote_copy(
            src_ref=start.at[s, :, :, pl.ds(top, HALO), :],
            dst_ref=start.at[s, :, :, pl.ds(low, HALO), :],
            send_sem=halo_s.at[0, s], recv_sem=halo_r.at[0, s],
            device_id={"lat": band - 1}, device_id_type=MESH,
        )

    def to_below(s):
        return pltpu.make_async_remote_copy(
            src_ref=start.at[s, :, :, pl.ds(low - HALO, HALO), :],
            dst_ref=start.at[s, :, :, pl.ds(0, HALO), :],
            send_sem=halo_s.at[1, s], recv_sem=halo_r.at[1, s],
            device_id={"lat": band + 1}, device_id_type=MESH,
        )

    def st_above():
        return pltpu.make_async_remote_copy(
            src_ref=st.at[:, pl.ds(0, wins), pl.ds(top, HALO), :], dst_ref=st.at[:, pl.ds(0, wins), pl.ds(low, HALO), :],
            send_sem=st_s.at[0], recv_sem=st_r.at[0],
            device_id={"lat": band - 1}, device_id_type=MESH,
        )

    def st_below():
        return pltpu.make_async_remote_copy(
            src_ref=st.at[:, pl.ds(0, wins), pl.ds(low - HALO, HALO), :], dst_ref=st.at[:, pl.ds(0, wins), pl.ds(0, HALO), :],
            send_sem=st_s.at[1], recv_sem=st_r.at[1],
            device_id={"lat": band + 1}, device_id_type=MESH,
        )

    def send_halo(s):
        @pl.when(up_ok)
        def _():
            to_above(s).start()

        @pl.when(down_ok)
        def _():
            to_below(s).start()

    def recv_halo(s):
        @pl.when(down_ok)
        def _():
            to_above(s).wait_recv()

        @pl.when(up_ok)
        def _():
            to_below(s).wait_recv()

    own.wait()
    send_halo(me)

    for n, (src, dst) in enumerate(singles):
        pltpu.make_async_copy(dst, dst, load_sem.at[1 + n]).wait()

    def prepare(r, _):
        at = pl.ds(pl.multiple_of(top + 8 * r, 8), 8)
        for c in range(wins + 1):
            sea = mask_win[c, pl.ds(pl.multiple_of(8 * r, 8), 8), :].astype(jnp.float32)
            st[1, c, at, :] = sea
            st[0, c, at, :] = st[0, c, at, :] * sea
        for a in range(4):
            st[a, per, at, :] = jnp.where(early, st[a, per, at, :], st[a, wins, at, :])
        return 0

    lax.fori_loop(0, rows // 8, prepare, 0)

    @pl.when(up_ok)
    def _():
        st_above().start()

    @pl.when(down_ok)
    def _():
        st_below().start()

    zero = jnp.zeros((8, 128), jnp.float32)

    def blank(first):
        def body(r, _):
            at = pl.ds(pl.multiple_of(first + 8 * r, 8), 8)
            for c in range(wins):
                for a in range(4):
                    st[a, c, at, :] = zero
                for s in range(sections):
                    for a in range(3):
                        start[s, c, a, at, :] = zero
            return 0

        lax.fori_loop(0, HALO // 8, body, 0)

    @pl.when(band == 0)
    def _():
        blank(0)

    @pl.when(band == bands - 1)
    def _():
        blank(low)

    def edge(lo, hi):
        for buf in (raised, flux):
            for c in range(wins):
                buf[c, pl.ds(8 * lo, 8), :] = zero
                buf[c, pl.ds(8 * hi + 8, 8), :] = zero

    acc[...] = jnp.zeros_like(acc)

    @pl.when(down_ok)
    def _():
        st_above().wait_recv()

    @pl.when(up_ok)
    def _():
        st_below().wait_recv()

    def lon_diff(xs, c):
        lane = lax.broadcasted_iota(jnp.int32, xs[c].shape, 1)
        after, before = xs[(c + 1) % wins], xs[c - 1]
        east_of = pltpu.roll(jnp.where(lane == 0, after, xs[c]), 127, 1)
        return east_of - pltpu.roll(jnp.where(lane == 127, before, xs[c]), 1, 1)

    def lon_diffs(xs):
        return [lon_diff(xs, c) for c in range(wins)]

    def lat_diff(ref, c, r0, high):
        return ref[c, pl.ds(r0 + 9, high), :] - ref[c, pl.ds(r0 + 7, high), :]

    def sweep(lo, hi, body):
        n = -(-(hi - lo) // STRIPS)
        size, more = divmod(hi - lo, n)
        at = lo
        for length, times in ((size + 1, more), (size, n - more)):
            if times:
                def turns(i, _, at=at, length=length):
                    r0 = pl.multiple_of(8 * (at + i * length), 8)
                    body(r0, 8 * length, pl.ds(r0, 8 * length), pl.ds(pl.multiple_of(r0 + 8, 8), 8 * length))
                    return 0

                lax.fori_loop(0, times, turns, 0)
                at += length * times

    def strip_sum(xs):
        return jnp.sum(sum(xs).reshape(-1, 8, 128), axis=0)

    def run(kind, source, s, lo, hi, finish, target_of=None):
        def push(h, c, at, step):
            if kind != "forced":
                return 0.5 * h
            base = 2 * (s * STEPS + step)
            return 0.5 * (h + (trig[base] * st[2, c, at, :] + trig[base + 1] * st[3, c, at, :]))

        def begin(r0, high_rows, at, padded):
            for c in range(wins):
                raised[c, padded, :] = push(source[s, c, 0, at, :], c, at, 0)

        sweep(lo, hi, begin)
        edge(lo, hi)

        def advance(step, is_first, is_last):
            def first(r0, high_rows, at, padded):
                slopes = lon_diffs([raised[c, padded, :] for c in range(wins)])
                cor = rows_in[0, at, :]
                for c in range(wins):
                    wet, sea = st[0, c, at, :], st[1, c, at, :]
                    dx, dy = slopes[c], lat_diff(raised, c, r0, high_rows)
                    if is_first:
                        u, v = source[s, c, 1, at, :], source[s, c, 2, at, :]
                    else:
                        u, v = east[c, at, :], north[c, at, :]
                    if kind == "back":
                        e = sea * (u + wet * dx)
                        f = sea * (v + wet * dy)
                        east[c, at, :] = DRAG_RATE * e - cor * f
                        north[c, at, :] = cor * e + DRAG_RATE * f
                        fluy[c, at, :], flux[c, padded, :] = 0.5 * e, 0.5 * f
                    else:
                        e = sea * (DRAG_RATE * u + cor * v - dx)
                        f = sea * (DRAG_RATE * v - cor * u - dy)
                        half = 0.5 * wet
                        east[c, at, :], north[c, at, :] = e, f
                        fluy[c, at, :], flux[c, padded, :] = half * e, half * f

            sweep(lo, hi, first)

            def second(r0, high_rows, at, padded):
                slopes = lon_diffs([fluy[c, at, :] for c in range(wins)])
                inside = rows_in[1, at, :]
                sums = []
                for c in range(wins):
                    d = slopes[c] + lat_diff(flux, c, r0, high_rows)
                    h = source[s, c, 0, at, :] if is_first else high[c, at, :]
                    h = (h + d if kind == "back" else h - d) * inside
                    if not is_last:
                        high[c, at, :], raised[c, padded, :] = h, push(h, c, at, step + 1)
                        continue
                    values = finish(c, at, (h, east[c, at, :], north[c, at, :]))
                    if kind == "free":
                        if c < per:
                            sums.append(values)
                    else:
                        target, slot = target_of
                        for a in range(3):
                            target[slot, c, a, at, :] = values[a]
                if sums:
                    acc[0] += strip_sum([x for x, _ in sums])
                    acc[1] += strip_sum([x for _, x in sums])

            inner = 1 if is_last else 0
            sweep(lo + inner, hi - inner, second)

        advance(0, True, False)

        def middle(step, _):
            advance(step, False, False)
            return 0

        lax.fori_loop(1, STEPS - 1, middle, 0)
        advance(STEPS - 1, False, True)

    def keep(c, at, values):
        return values

    def arrive(n):
        s = turn(n)
        piece(s, s).wait_recv()
        send_halo(s)

    def forced(n, _):
        @pl.when(n == 1)
        def _():
            for i in range(1, sections - 1):
                piece(turn(i), me).wait_send()
            piece(turn(sections - 1), me).start()
            for i in range(1, sections - 1):
                arrive(i)

        @pl.when(n == sections - 2)
        def _():
            arrive(sections - 1)

        s = turn(n)
        recv_halo(s)
        run("forced", start, s, 0, strips, keep, (mis, s))
        return 0

    lax.fori_loop(0, sections, forced, 0)

    def subtract(s, after):
        def body(r, _):
            at = pl.ds(pl.multiple_of(8 * r, 8), 8)
            out = [
                [mis[s, c, a, at, :] - start[after, c, a, at, :] for a in range(3)]
                for c in range(wins)
            ]
            for c in range(wins):
                for a in range(3):
                    mis[s, c, a, at, :] = out[c][a]
            return 0

        lax.fori_loop(1, strips - 1, body, 0)

    subtract(me, peer(1))
    columns = pl.ds(me * per, per)
    own_mis = pltpu.make_async_copy(
        mis.at[me, pl.ds(0, per), :, pl.ds(top, rows), :],
        home.at[columns],
        own_sem.at[1],
    )
    own_mis.start()

    def give(source, target, send, recv, s, at_columns, slot):
        return pltpu.make_async_remote_copy(
            src_ref=source.at[s, pl.ds(0, per), :, pl.ds(top, rows), :],
            dst_ref=target.at[at_columns],
            send_sem=send.at[s], recv_sem=recv.at[slot],
            device_id={"sec": s}, device_id_type=MESH,
        )

    def differ(i, _):
        s = peer(i)
        subtract(s, peer(i + 1))
        give(mis, home, s2, r2, s, columns, me).start()
        return 0

    lax.fori_loop(1, sections, differ, 0)

    def back(i, _):
        s = peer(i)
        before = peer(i + sections - 1)

        def done(c, at, values):
            return [x - mis[before, c, a, at, :] for a, x in enumerate(values)]

        run("back", mis, s, 1, strips - 1, done, (grad, s))

        @pl.when(i < sections)
        def _():
            give(grad, full, s3, r3, s, columns, me).start()

        return 0

    lax.fori_loop(1, sections + 1, back, 0)
    own_grad = pltpu.make_async_copy(
        grad.at[me, pl.ds(0, per), :, pl.ds(top, rows), :],
        full.at[columns],
        own_sem.at[2],
    )
    own_grad.start()

    def image(i, _):
        s = peer(i)
        after = peer(i + 1)

        def squares(c, at, values):
            pairs = [(x, grad[after, c, a, at, :]) for a, x in enumerate(values)]
            return sum(g * g for _, g in pairs), sum((x - g) * (x - g) for x, g in pairs)

        run("free", grad, s, 2, strips - 2, squares)
        return 0

    lax.fori_loop(0, sections, image, 0)

    part[me] = acc[...]

    def share_part(j, slot):
        return pltpu.make_async_remote_copy(
            src_ref=acc, dst_ref=part.at[slot], send_sem=ps.at[j], recv_sem=pr.at[slot],
            device_id={"sec": j}, device_id_type=MESH,
        )

    for i in range(1, sections):
        share_part(peer(i), me).start()
    for i in range(1, sections):
        share_part(peer(i), peer(i)).wait_recv()
    for i in range(1, sections):
        share_part(peer(i), me).wait_send()
    summed = part[0]
    for s in range(1, sections):
        summed = summed + part[s]
    acc[...] = summed
    total[band] = summed

    def share_total(j, slot):
        return pltpu.make_async_remote_copy(
            src_ref=acc, dst_ref=total.at[slot], send_sem=ts.at[j], recv_sem=tr.at[slot],
            device_id={"lat": j}, device_id_type=MESH,
        )

    for i in range(1, bands):
        share_total(lax.rem(band + i, bands), band).start()
    for i in range(1, bands):
        j = lax.rem(band + i, bands)
        share_total(j, j).wait_recv()
    summed = total[0]
    for s in range(1, bands):
        summed = summed + total[s]
    sums = jnp.sum(jnp.sum(summed, axis=2, keepdims=True), axis=1, keepdims=True)
    step = sums[0] / count / (sums[1] / count + EPSILON)
    step_out[...] = jnp.broadcast_to(step, (8, 128))

    own_mis.wait()

    def mismatches(i, _):
        s = peer(i)
        give(mis, home, s2, r2, s, columns, s).wait()
        return 0

    lax.fori_loop(1, sections, mismatches, 0)

    own_grad.wait()

    def grads(i, _):
        s = peer(i)
        give(grad, full, s3, r3, s, columns, s).wait_recv()
        return 0

    lax.fori_loop(1, sections, grads, 0)


    piece(turn(sections - 1), me).wait_send()

    def drain(i, _):
        s = peer(i)
        give(grad, full, s3, r3, s, columns, me).wait_send()
        return 0

    lax.fori_loop(1, sections, drain, 0)

    def drain_halo(i, _):
        s = peer(i)

        @pl.when(up_ok)
        def _():
            to_above(s).wait_send()

        @pl.when(down_ok)
        def _():
            to_below(s).wait_send()

        return 0

    lax.fori_loop(0, sections, drain_halo, 0)

    @pl.when(up_ok)
    def _():
        st_above().wait_send()

    @pl.when(down_ok)
    def _():
        st_below().wait_send()

    for i in range(1, bands):
        share_total(lax.rem(band + i, bands), band).wait_send()


def finish_kernel(fields, home, full, step, new_fields, mismatch):
    rows, share = fields.shape[1:]
    length = step[0:1, :]

    def body(r, _):
        at = pl.ds(pl.multiple_of(8 * r, 8), 8)
        for c in range(share // 128):
            cols = slice(c * 128, c * 128 + 128)
            for a in range(3):
                new_fields[a, at, cols] = fields[a, at, cols] - length * full[c, a, at, :]
                mismatch[a, at, cols] = home[c, a, at, :]
        return 0

    lax.fori_loop(0, rows // 8, body, 0)


def shards(states, depth_field, land_mask, tide_cos, tide_sin):
    fields = states[0]
    rows, lon = fields.shape[1:]
    sections, bands = lax.axis_size("sec"), lax.axis_size("lat")
    band = lax.axis_index("lat")
    share = lon // sections
    tall = rows + 2 * HALO
    lat_total = rows * bands
    ids = band * rows - HALO + jnp.arange(tall, dtype=jnp.int32)
    inside = ((ids >= 0) & (ids < lat_total)).astype(jnp.float32)
    coriolis = CORIOLIS_MAX * jnp.sin(
        jnp.pi * (ids.astype(jnp.float32) + 0.5) / lat_total - 0.5 * jnp.pi
    )
    rows_in = jnp.broadcast_to(jnp.stack([coriolis, inside])[:, :, None], (2, tall, 128))
    angles = np.float32(TWO_PI) * np.arange(sections * STEPS, dtype=np.float32) / np.float32(
        sections * STEPS
    )
    trig = jnp.asarray(np.stack([np.cos(angles), np.sin(angles)], axis=1).reshape(-1))
    f32 = jnp.float32
    dma = pltpu.SemaphoreType.DMA
    any_spec = pl.BlockSpec(memory_space=pl.ANY)
    vmem = pl.BlockSpec(memory_space=pltpu.VMEM)
    tiles, wins = lon // 128, share // 128 + 1
    stacked = pltpu.VMEM((sections, wins, 3, tall, 128), f32)
    plain = pltpu.VMEM((wins, tall, 128), f32)
    padded = pltpu.VMEM((wins, tall + 16, 128), f32)
    gathered = jax.ShapeDtypeStruct((tiles, 3, rows, 128), f32)
    home, full, step = pl.pallas_call(
        functools.partial(kernel, sections, bands, float(sections * 3 * lat_total * lon)),
        out_shape=(
            gathered,
            gathered,
            jax.ShapeDtypeStruct((8, 128), f32),
        ),
        in_specs=[any_spec] * 5 + [vmem, pl.BlockSpec(memory_space=pltpu.SMEM)],
        out_specs=(any_spec, any_spec, vmem),
        scratch_shapes=[
            pltpu.VMEM((tiles + sections, 3, rows, 128), f32),
            pltpu.VMEM((wins + 1, rows, 128), jnp.int32),
            pltpu.VMEM((4, wins + 1, tall, 128), f32),
            stacked, stacked, stacked,
            plain, plain, plain, padded, padded, plain,
            pltpu.VMEM((2, 8, 128), f32),
            pltpu.VMEM((sections, 2, 8, 128), f32),
            pltpu.VMEM((bands, 2, 8, 128), f32),
            dma((5,)),
            dma((sections,)), dma((sections,)),
            dma((2, sections)), dma((2, sections)),
            dma((2,)), dma((2,)),
            dma((sections,)), dma((sections,)),
            dma((sections,)), dma((sections,)),
            dma((3,)),
            dma((sections,)), dma((sections,)),
            dma((bands,)), dma((bands,)),
        ],
        compiler_params=pltpu.CompilerParams(
            collective_id=0, has_side_effects=True, vmem_limit_bytes=60 * 1024 * 1024
        ),
        name="shooting",
    )(fields, depth_field, land_mask, tide_cos, tide_sin, rows_in, trig)
    block = pl.BlockSpec((3, rows, share), lambda i: (0, 0, i))
    by_tile = pl.BlockSpec((share // 128, 3, rows, 128), lambda i: (i, 0, 0, 0))
    new_fields, mismatch = pl.pallas_call(
        finish_kernel,
        grid=(sections,),
        out_shape=(jax.ShapeDtypeStruct(fields.shape, f32),) * 2,
        in_specs=[block, by_tile, by_tile, pl.BlockSpec((8, 128), lambda i: (0, 0))],
        out_specs=(block, block),
        compiler_params=pltpu.CompilerParams(vmem_limit_bytes=32 * 1024 * 1024),
        name="update",
    )(fields, home, full, step)
    return new_fields[None], mismatch[None], step[0, 0]


def solution(mesh):
    return jax.shard_map(
        shards,
        mesh=mesh,
        in_specs=(
            P("sec", None, "lat", None),
            P("lat", None),
            P("lat", None),
            P("lat", None),
            P("lat", None),
        ),
        out_specs=(P("sec", None, "lat", None), P("sec", None, "lat", None), P()),
        check_vma=False,
    )
```

```python
import functools
import math

import jax
import jax.numpy as jnp
import numpy as np
from jax import lax
from jax.experimental import pallas as pl
from jax.experimental.pallas import tpu as pltpu
from jax.sharding import PartitionSpec as P

STEPS = 4
DRAG_RATE = 0.9
CORIOLIS_MAX = 0.3
EPSILON = 1e-06
TWO_PI = 2.0 * math.pi
HALO = 24
STRIPS = 7
MESH = pl.DeviceIdType.MESH


def kernel(
    sections, bands, count,
    states, depth, mask, tide_one, tide_two, row_table, trig,
    home, full, step_out,
    plain, plain_st, plain_mask, rows_in, wide, st, start, mis, grad,
    high, east, north, raised, flux, fluy, acc, part, total,
    load_sem, s1, r1, halo_s, halo_r, st_s, st_r, s2, r2, s3, r3, own_sem, ps, pr, ts, tr,
):
    me = lax.axis_index("sec")
    band = lax.axis_index("lat")
    rows, lon = states.shape[1], states.shape[2]
    share = lon // sections
    per, tiles = share // 128, lon // 128
    wins = per + 1
    tall = rows + 2 * HALO
    strips = tall // 8
    top, low = HALO, HALO + rows

    def peer(i):
        return lax.rem(me + i, sections)

    def tile(c):
        return pl.ds(pl.multiple_of(c * 128, 128), 128)

    pltpu.make_async_copy(states, plain, load_sem.at[0]).start()
    singles = (
        (depth, plain_st.at[0]), (mask, plain_mask), (tide_one, plain_st.at[1]), (tide_two, plain_st.at[2])
    )
    ends = (
        (pl.ds(pl.multiple_of(me * share, 128), share), pl.ds(0, share)),
        (tile(lax.rem(me * per + per, tiles)), pl.ds(share, 128)),
        (tile(lax.rem(me * per + tiles - 1, tiles)), pl.ds(share + 128, 128)),
    )
    for n, (src, dst) in enumerate(singles):
        for there, here in ends:
            pltpu.make_async_copy(src.at[:, there], dst.at[:, here], load_sem.at[1 + n]).start()
    table = row_table.at[:, pl.ds(pl.multiple_of(band * rows, 8), tall), :]
    pltpu.make_async_copy(table, rows_in, load_sem.at[5]).start()

    barrier = pltpu.get_barrier_semaphore()
    for i in range(1, sections):
        pl.semaphore_signal(barrier, inc=1, device_id={"sec": peer(i)}, device_id_type=MESH)
    for i in range(1, bands):
        pl.semaphore_signal(
            barrier, inc=1, device_id={"lat": lax.rem(band + i, bands)}, device_id_type=MESH
        )
    pl.semaphore_wait(barrier, sections + bands - 2)

    pltpu.make_async_copy(states, plain, load_sem.at[0]).wait()
    early = lax.broadcasted_iota(jnp.int32, (8, 128), 1) < 64

    def pack(j, write):
        def body(r, _):
            r0 = pl.multiple_of(8 * r, 8)
            at = pl.ds(r0, 8)
            for a in range(3):
                for c in range(per):
                    write(c, a, r0, plain[a, at, tile(j * per + c)])
                after = plain[a, at, tile(lax.rem(j * per + per, tiles))]
                before = plain[a, at, tile(lax.rem(j * per + tiles - 1, tiles))]
                write(per, a, r0, jnp.where(early, after, before))
            return 0

        lax.fori_loop(0, rows // 8, body, 0)

    def piece(j, slot):
        return pltpu.make_async_remote_copy(
            src_ref=wide.at[j],
            dst_ref=start.at[me, :, :, pl.ds(top, rows), :],
            send_sem=s1.at[j],
            recv_sem=r1.at[slot],
            device_id={"sec": j},
            device_id_type=MESH,
        )

    def turn(n):
        return lax.rem(me + jnp.where(lax.rem(me, 2) == 0, n, sections - n), sections)

    def pack_piece(n, _):
        j = turn(n)

        def write(c, a, r0, x):
            wide[j, c, a, pl.ds(r0, 8), :] = x

        pack(j, write)

        @pl.when(n < sections - 1)
        def _():
            piece(j, me).start()

        return 0

    lax.fori_loop(1, sections, pack_piece, 0)

    def write_own(c, a, r0, x):
        start[me, c, a, pl.ds(pl.multiple_of(top + r0, 8), 8), :] = x

    pack(me, write_own)

    up_ok, down_ok = band > 0, band < bands - 1

    def to_above(s):
        return pltpu.make_async_remote_copy(
            src_ref=start.at[s, :, :, pl.ds(top, HALO), :],
            dst_ref=start.at[s, :, :, pl.ds(low, HALO), :],
            send_sem=halo_s.at[0, s], recv_sem=halo_r.at[0, s],
            device_id={"lat": band - 1}, device_id_type=MESH,
        )

    def to_below(s):
        return pltpu.make_async_remote_copy(
            src_ref=start.at[s, :, :, pl.ds(low - HALO, HALO), :],
            dst_ref=start.at[s, :, :, pl.ds(0, HALO), :],
            send_sem=halo_s.at[1, s], recv_sem=halo_r.at[1, s],
            device_id={"lat": band + 1}, device_id_type=MESH,
        )

    def st_above():
        return pltpu.make_async_remote_copy(
            src_ref=st.at[:, :, pl.ds(top, HALO), :], dst_ref=st.at[:, :, pl.ds(low, HALO), :],
            send_sem=st_s.at[0], recv_sem=st_r.at[0],
            device_id={"lat": band - 1}, device_id_type=MESH,
        )

    def st_below():
        return pltpu.make_async_remote_copy(
            src_ref=st.at[:, :, pl.ds(low - HALO, HALO), :], dst_ref=st.at[:, :, pl.ds(0, HALO), :],
            send_sem=st_s.at[1], recv_sem=st_r.at[1],
            device_id={"lat": band + 1}, device_id_type=MESH,
        )

    def send_halo(s):
        @pl.when(up_ok)
        def _():
            to_above(s).start()

        @pl.when(down_ok)
        def _():
            to_below(s).start()

    def recv_halo(s):
        @pl.when(down_ok)
        def _():
            to_above(s).wait_recv()

        @pl.when(up_ok)
        def _():
            to_below(s).wait_recv()

    send_halo(me)

    for n, (src, dst) in enumerate(singles):
        pltpu.make_async_copy(dst, dst, load_sem.at[1 + n]).wait()

    def prepare(r, _):
        r0 = pl.multiple_of(8 * r, 8)
        at, to = pl.ds(r0, 8), pl.ds(pl.multiple_of(top + r0, 8), 8)
        for c in range(wins):
            def window(ref):
                x = ref[at, c * 128 : c * 128 + 128]
                if c == per:
                    x = jnp.where(early, x, ref[at, c * 128 + 128 : c * 128 + 256])
                return x.astype(jnp.float32)

            sea = window(plain_mask)
            st[0, c, to, :] = window(plain_st.at[0]) * sea
            st[1, c, to, :] = sea
            st[2, c, to, :] = window(plain_st.at[1])
            st[3, c, to, :] = window(plain_st.at[2])
        return 0

    lax.fori_loop(0, rows // 8, prepare, 0)

    @pl.when(up_ok)
    def _():
        st_above().start()

    @pl.when(down_ok)
    def _():
        st_below().start()

    zero = jnp.zeros((8, 128), jnp.float32)

    def blank(first):
        def body(r, _):
            at = pl.ds(pl.multiple_of(first + 8 * r, 8), 8)
            for c in range(wins):
                for a in range(4):
                    st[a, c, at, :] = zero
                for s in range(sections):
                    for a in range(3):
                        start[s, c, a, at, :] = zero
            return 0

        lax.fori_loop(0, HALO // 8, body, 0)

    @pl.when(band == 0)
    def _():
        blank(0)

    @pl.when(band == bands - 1)
    def _():
        blank(low)

    def edge(lo, hi):
        for buf in (raised, flux):
            for c in range(wins):
                buf[c, pl.ds(8 * lo, 8), :] = zero
                buf[c, pl.ds(8 * hi + 8, 8), :] = zero

    acc[...] = jnp.zeros_like(acc)
    pltpu.make_async_copy(table, rows_in, load_sem.at[5]).wait()

    @pl.when(down_ok)
    def _():
        st_above().wait_recv()

    @pl.when(up_ok)
    def _():
        st_below().wait_recv()

    def lon_diff(xs, c):
        lane = lax.broadcasted_iota(jnp.int32, xs[c].shape, 1)
        after, before = xs[(c + 1) % wins], xs[c - 1]
        east_of = pltpu.roll(jnp.where(lane == 0, after, xs[c]), 127, 1)
        return east_of - pltpu.roll(jnp.where(lane == 127, before, xs[c]), 1, 1)

    def lon_diffs(xs):
        return [lon_diff(xs, c) for c in range(wins)]

    def lat_diff(ref, c, r0, high):
        return ref[c, pl.ds(r0 + 9, high), :] - ref[c, pl.ds(r0 + 7, high), :]

    def sweep(lo, hi, body):
        n = -(-(hi - lo) // STRIPS)
        size, more = divmod(hi - lo, n)
        at = lo
        for length, times in ((size + 1, more), (size, n - more)):
            if times:
                def turns(i, _, at=at, length=length):
                    r0 = pl.multiple_of(8 * (at + i * length), 8)
                    body(r0, 8 * length, pl.ds(r0, 8 * length), pl.ds(pl.multiple_of(r0 + 8, 8), 8 * length))
                    return 0

                lax.fori_loop(0, times, turns, 0)
                at += length * times

    def strip_sum(xs):
        return jnp.sum(sum(xs).reshape(-1, 8, 128), axis=0)

    def run(kind, source, s, lo, hi, finish, target_of=None):
        def push(h, c, at, step):
            if kind != "forced":
                return 0.5 * h
            base = 2 * (s * STEPS + step)
            return 0.5 * (h + (trig[base] * st[2, c, at, :] + trig[base + 1] * st[3, c, at, :]))

        def begin(r0, high_rows, at, padded):
            for c in range(wins):
                raised[c, padded, :] = push(source[s, c, 0, at, :], c, at, 0)

        sweep(lo, hi, begin)
        edge(lo, hi)

        def advance(step, is_first, is_last):
            def first(r0, high_rows, at, padded):
                slopes = lon_diffs([raised[c, padded, :] for c in range(wins)])
                cor = rows_in[0, at, :]
                for c in range(wins):
                    wet, sea = st[0, c, at, :], st[1, c, at, :]
                    dx, dy = slopes[c], lat_diff(raised, c, r0, high_rows)
                    if is_first:
                        u, v = source[s, c, 1, at, :], source[s, c, 2, at, :]
                    else:
                        u, v = east[c, at, :], north[c, at, :]
                    if kind == "back":
                        e = sea * (u + wet * dx)
                        f = sea * (v + wet * dy)
                        east[c, at, :] = DRAG_RATE * e - cor * f
                        north[c, at, :] = cor * e + DRAG_RATE * f
                        fluy[c, at, :], flux[c, padded, :] = 0.5 * e, 0.5 * f
                    else:
                        e = sea * (DRAG_RATE * u + cor * v - dx)
                        f = sea * (DRAG_RATE * v - cor * u - dy)
                        half = 0.5 * wet
                        east[c, at, :], north[c, at, :] = e, f
                        fluy[c, at, :], flux[c, padded, :] = half * e, half * f

            sweep(lo, hi, first)

            def second(r0, high_rows, at, padded):
                slopes = lon_diffs([fluy[c, at, :] for c in range(wins)])
                inside = rows_in[1, at, :]
                sums = []
                for c in range(wins):
                    d = slopes[c] + lat_diff(flux, c, r0, high_rows)
                    h = source[s, c, 0, at, :] if is_first else high[c, at, :]
                    h = (h + d if kind == "back" else h - d) * inside
                    if not is_last:
                        high[c, at, :], raised[c, padded, :] = h, push(h, c, at, step + 1)
                        continue
                    values = finish(c, at, (h, east[c, at, :], north[c, at, :]))
                    if kind == "free":
                        if c < per:
                            sums.append(values)
                    else:
                        target, slot = target_of
                        for a in range(3):
                            target[slot, c, a, at, :] = values[a]
                if sums:
                    acc[0] += strip_sum([x for x, _ in sums])
                    acc[1] += strip_sum([x for _, x in sums])

            inner = 1 if is_last else 0
            sweep(lo + inner, hi - inner, second)

        advance(0, True, False)

        def middle(step, _):
            advance(step, False, False)
            return 0

        lax.fori_loop(1, STEPS - 1, middle, 0)
        advance(STEPS - 1, False, True)

    def keep(c, at, values):
        return values

    def arrive(n):
        s = turn(n)
        piece(s, s).wait_recv()
        send_halo(s)

    def subtract(s, first_strip, last_strip):
        after = lax.rem(s + 1, sections)
        at = pl.ds(8 * first_strip, 8 * (last_strip - first_strip))

        def body(c, _):
            for a in range(3):
                mis[s, c, a, at, :] = mis[s, c, a, at, :] - start[after, c, a, at, :]
            return 0

        lax.fori_loop(0, wins, body, 0)

    columns = pl.ds(me * per, per)

    def give(source, target, send, recv, s, at_columns, slot):
        return pltpu.make_async_remote_copy(
            src_ref=source.at[s, pl.ds(0, per), :, pl.ds(top, rows), :],
            dst_ref=target.at[at_columns],
            send_sem=send.at[s], recv_sem=recv.at[slot],
            device_id={"sec": s}, device_id_type=MESH,
        )

    def send_mismatch(n):
        subtract(turn(n), top // 8, low // 8)
        give(mis, home, s2, r2, turn(n), columns, me).start()

    even = lax.rem(me, 2) == 0

    def forced(n, _):
        @pl.when(n == 1)
        def _():
            for i in range(1, sections - 1):
                piece(turn(i), me).wait_send()
            piece(turn(sections - 1), me).start()
            for i in range(1, sections - 1):
                arrive(i)

        s = turn(n)
        recv_halo(s)
        run("forced", start, s, 0, strips, keep, (mis, s))

        late = jnp.logical_and(n == sections - 2, even)

        @pl.when(jnp.logical_and(n > 0, jnp.logical_not(late)))
        def _():
            send_mismatch(n)

        @pl.when(n == sections - 2)
        def _():
            arrive(sections - 1)

        @pl.when(late)
        def _():
            send_mismatch(n)

        return 0

    lax.fori_loop(0, sections, forced, 0)
    subtract(me, top // 8, low // 8)
    own_mis = pltpu.make_async_copy(
        mis.at[me, pl.ds(0, per), :, pl.ds(top, rows), :],
        home.at[columns],
        own_sem.at[1],
    )
    own_mis.start()

    def fringe(s, _):
        subtract(s, 1, top // 8)
        subtract(s, low // 8, strips - 1)
        return 0

    lax.fori_loop(0, sections, fringe, 0)

    def back(i, _):
        s = turn(lax.rem(i, sections))
        before = lax.rem(s + sections - 1, sections)

        def done(c, at, values):
            return [x - mis[before, c, a, at, :] for a, x in enumerate(values)]

        run("back", mis, s, 1, strips - 1, done, (grad, s))

        @pl.when(i < sections)
        def _():
            give(grad, full, s3, r3, s, columns, me).start()

        return 0

    lax.fori_loop(1, sections + 1, back, 0)
    own_grad = pltpu.make_async_copy(
        grad.at[me, pl.ds(0, per), :, pl.ds(top, rows), :],
        full.at[columns],
        own_sem.at[2],
    )
    own_grad.start()

    def image(i, _):
        s = peer(i)
        after = peer(i + 1)

        def squares(c, at, values):
            pairs = [(x, grad[after, c, a, at, :]) for a, x in enumerate(values)]
            return sum(g * g for _, g in pairs), sum((x - g) * (x - g) for x, g in pairs)

        run("free", grad, s, 2, strips - 2, squares)
        return 0

    lax.fori_loop(0, sections, image, 0)

    part[me] = acc[...]

    def share_part(j, slot):
        return pltpu.make_async_remote_copy(
            src_ref=acc, dst_ref=part.at[slot], send_sem=ps.at[j], recv_sem=pr.at[slot],
            device_id={"sec": j}, device_id_type=MESH,
        )

    for i in range(1, sections):
        share_part(peer(i), me).start()
    for i in range(1, sections):
        share_part(peer(i), peer(i)).wait_recv()
    for i in range(1, sections):
        share_part(peer(i), me).wait_send()
    summed = part[0]
    for s in range(1, sections):
        summed = summed + part[s]
    acc[...] = summed
    total[band] = summed

    def share_total(j, slot):
        return pltpu.make_async_remote_copy(
            src_ref=acc, dst_ref=total.at[slot], send_sem=ts.at[j], recv_sem=tr.at[slot],
            device_id={"lat": j}, device_id_type=MESH,
        )

    for i in range(1, bands):
        share_total(lax.rem(band + i, bands), band).start()
    for i in range(1, bands):
        j = lax.rem(band + i, bands)
        share_total(j, j).wait_recv()
    summed = total[0]
    for s in range(1, bands):
        summed = summed + total[s]
    sums = jnp.sum(jnp.sum(summed, axis=2, keepdims=True), axis=1, keepdims=True)
    step = sums[0] / count / (sums[1] / count + EPSILON)
    step_out[...] = jnp.broadcast_to(step, (8, 128))

    own_mis.wait()

    def mismatches(i, _):
        s = peer(i)
        give(mis, home, s2, r2, s, columns, s).wait()
        return 0

    lax.fori_loop(1, sections, mismatches, 0)

    own_grad.wait()

    def grads(i, _):
        s = peer(i)
        give(grad, full, s3, r3, s, columns, s).wait_recv()
        return 0

    lax.fori_loop(1, sections, grads, 0)


    piece(turn(sections - 1), me).wait_send()

    def drain(i, _):
        s = peer(i)
        give(grad, full, s3, r3, s, columns, me).wait_send()
        return 0

    lax.fori_loop(1, sections, drain, 0)

    def drain_halo(i, _):
        s = peer(i)

        @pl.when(up_ok)
        def _():
            to_above(s).wait_send()

        @pl.when(down_ok)
        def _():
            to_below(s).wait_send()

        return 0

    lax.fori_loop(0, sections, drain_halo, 0)

    @pl.when(up_ok)
    def _():
        st_above().wait_send()

    @pl.when(down_ok)
    def _():
        st_below().wait_send()

    for i in range(1, bands):
        share_total(lax.rem(band + i, bands), band).wait_send()


def finish_kernel(fields, home, full, step, new_fields, mismatch):
    rows, width = fields.shape[1:]
    length = step[0:1, :]

    def body(r, _):
        at = pl.ds(pl.multiple_of(8 * r, 8), 8)
        for c in range(width // 128):
            cols = slice(c * 128, c * 128 + 128)
            for a in range(3):
                new_fields[a, at, cols] = fields[a, at, cols] - length * full[c, a, at, :]
                mismatch[a, at, cols] = home[c, a, at, :]
        return 0

    lax.fori_loop(0, rows // 8, body, 0)


def shards(states, depth_field, land_mask, tide_cos, tide_sin):
    fields = states[0]
    rows, lon = fields.shape[1:]
    sections, bands = lax.axis_size("sec"), lax.axis_size("lat")
    share = lon // sections
    tall = rows + 2 * HALO
    lat_total = rows * bands
    ids = np.arange(lat_total + 2 * HALO, dtype=np.float32) - HALO
    inside = ((ids >= 0) & (ids < lat_total)).astype(np.float32)
    turned = np.float32(math.pi) * (ids + np.float32(0.5)) / np.float32(lat_total)
    coriolis = np.float32(CORIOLIS_MAX) * np.sin(turned - np.float32(0.5 * math.pi))
    row_table = np.broadcast_to(np.stack([coriolis, inside])[:, :, None], (2, ids.size, 128))
    row_table = jnp.asarray(row_table.astype(np.float32))
    angles = np.float32(TWO_PI) * np.arange(sections * STEPS, dtype=np.float32) / np.float32(
        sections * STEPS
    )
    trig = jnp.asarray(np.stack([np.cos(angles), np.sin(angles)], axis=1).reshape(-1))
    f32 = jnp.float32
    dma = pltpu.SemaphoreType.DMA
    any_spec = pl.BlockSpec(memory_space=pl.ANY)
    vmem = pl.BlockSpec(memory_space=pltpu.VMEM)
    tiles, wins = lon // 128, share // 128 + 1
    stacked = pltpu.VMEM((sections, wins, 3, tall, 128), f32)
    plain = pltpu.VMEM((wins, tall, 128), f32)
    padded = pltpu.VMEM((wins, tall + 16, 128), f32)
    gathered = jax.ShapeDtypeStruct((tiles, 3, rows, 128), f32)
    home, full, step = pl.pallas_call(
        functools.partial(kernel, sections, bands, float(sections * 3 * lat_total * lon)),
        out_shape=(
            gathered,
            gathered,
            jax.ShapeDtypeStruct((8, 128), f32),
        ),
        in_specs=[any_spec] * 6 + [pl.BlockSpec(memory_space=pltpu.SMEM)],
        out_specs=(any_spec, any_spec, vmem),
        scratch_shapes=[
            pltpu.VMEM((3, rows, lon), f32),
            pltpu.VMEM((3, rows, share + 256), f32),
            pltpu.VMEM((rows, share + 256), jnp.int32),
            pltpu.VMEM((2, tall, 128), f32),
            pltpu.VMEM((sections, wins, 3, rows, 128), f32),
            pltpu.VMEM((4, wins, tall, 128), f32),
            stacked, stacked, stacked,
            plain, plain, plain, padded, padded, plain,
            pltpu.VMEM((2, 8, 128), f32),
            pltpu.VMEM((sections, 2, 8, 128), f32),
            pltpu.VMEM((bands, 2, 8, 128), f32),
            dma((6,)),
            dma((sections,)), dma((sections,)),
            dma((2, sections)), dma((2, sections)),
            dma((2,)), dma((2,)),
            dma((sections,)), dma((sections,)),
            dma((sections,)), dma((sections,)),
            dma((3,)),
            dma((sections,)), dma((sections,)),
            dma((bands,)), dma((bands,)),
        ],
        compiler_params=pltpu.CompilerParams(
            collective_id=0, has_side_effects=True, vmem_limit_bytes=60 * 1024 * 1024
        ),
        name="shooting",
    )(fields, depth_field, land_mask, tide_cos, tide_sin, row_table, trig)
    half = share // 2
    block = pl.BlockSpec((3, rows, half), lambda i: (0, 0, i))
    by_tile = pl.BlockSpec((half // 128, 3, rows, 128), lambda i: (i, 0, 0, 0))
    new_fields, mismatch = pl.pallas_call(
        finish_kernel,
        grid=(2 * sections,),
        out_shape=(jax.ShapeDtypeStruct(fields.shape, f32),) * 2,
        in_specs=[block, by_tile, by_tile, pl.BlockSpec((8, 128), lambda i: (0, 0))],
        out_specs=(block, block),
        compiler_params=pltpu.CompilerParams(vmem_limit_bytes=60 * 1024 * 1024),
        name="update",
    )(fields, home, full, step)
    return new_fields[None], mismatch[None], step[0, 0]


def solution(mesh):
    return jax.shard_map(
        shards,
        mesh=mesh,
        in_specs=(
            P("sec", None, "lat", None),
            P("lat", None),
            P("lat", None),
            P("lat", None),
            P("lat", None),
        ),
        out_specs=(P("sec", None, "lat", None), P("sec", None, "lat", None), P()),
        check_vma=False,
    )
```

```python
import functools
import math

import jax
import jax.numpy as jnp
import numpy as np
from jax import lax
from jax.experimental import pallas as pl
from jax.experimental.pallas import tpu as pltpu
from jax.sharding import PartitionSpec as P

STEPS = 4
DRAG_RATE = 0.9
CORIOLIS_MAX = 0.3
EPSILON = 1e-06
TWO_PI = 2.0 * math.pi
HALO = 24
STRIPS = 7
MESH = pl.DeviceIdType.MESH


def kernel(
    sections, bands, count,
    states, depth, mask, tide_one, tide_two, row_table, trig,
    home, full, step_out,
    plain, plain_st, plain_mask, rows_in, wide, st, start, mis, grad,
    high, east, north, raised, flux, fluy, acc, part, total,
    load_sem, s1, r1, halo_s, halo_r, st_s, st_r, s2, r2, s3, r3, own_sem, ps, pr, ts, tr,
):
    me = lax.axis_index("sec")
    band = lax.axis_index("lat")
    rows, lon = states.shape[1], states.shape[2]
    share = lon // sections
    per, tiles = share // 128, lon // 128
    wins = per + 1
    tall = rows + 2 * HALO
    strips = tall // 8
    top, low = HALO, HALO + rows

    def peer(i):
        return lax.rem(me + i, sections)

    def tile(c):
        return pl.ds(pl.multiple_of(c * 128, 128), 128)

    barrier = pltpu.get_barrier_semaphore()
    for i in range(1, sections):
        pl.semaphore_signal(barrier, inc=1, device_id={"sec": peer(i)}, device_id_type=MESH)
    for i in range(1, bands):
        pl.semaphore_signal(
            barrier, inc=1, device_id={"lat": lax.rem(band + i, bands)}, device_id_type=MESH
        )
    pltpu.make_async_copy(states, plain, load_sem.at[0]).start()
    singles = (
        (depth, plain_st.at[0]), (mask, plain_mask), (tide_one, plain_st.at[1]), (tide_two, plain_st.at[2])
    )
    ends = (
        (pl.ds(pl.multiple_of(me * share, 128), share), pl.ds(0, share)),
        (tile(lax.rem(me * per + per, tiles)), pl.ds(share, 128)),
        (tile(lax.rem(me * per + tiles - 1, tiles)), pl.ds(share + 128, 128)),
    )
    for n, (src, dst) in enumerate(singles):
        for there, here in ends:
            pltpu.make_async_copy(src.at[:, there], dst.at[:, here], load_sem.at[1 + n]).start()
    table = row_table.at[:, pl.ds(pl.multiple_of(band * rows, 8), tall), :]
    pltpu.make_async_copy(table, rows_in, load_sem.at[5]).start()

    pltpu.make_async_copy(states, plain, load_sem.at[0]).wait()
    early = lax.broadcasted_iota(jnp.int32, (8, 128), 1) < 64

    def pack(j, write):
        def body(r, _):
            r0 = pl.multiple_of(8 * r, 8)
            at = pl.ds(r0, 8)
            for a in range(3):
                for c in range(per):
                    write(c, a, r0, plain[a, at, tile(j * per + c)])
                after = plain[a, at, tile(lax.rem(j * per + per, tiles))]
                before = plain[a, at, tile(lax.rem(j * per + tiles - 1, tiles))]
                write(per, a, r0, jnp.where(early, after, before))
            return 0

        lax.fori_loop(0, rows // 8, body, 0)

    def piece(j, slot):
        return pltpu.make_async_remote_copy(
            src_ref=wide.at[j],
            dst_ref=start.at[me, :, :, pl.ds(top, rows), :],
            send_sem=s1.at[j],
            recv_sem=r1.at[slot],
            device_id={"sec": j},
            device_id_type=MESH,
        )

    def turn(n):
        return lax.rem(me + jnp.where(lax.rem(me, 2) == 0, n, sections - n), sections)

    def pack_piece(n, _):
        j = turn(n)

        def write(c, a, r0, x):
            wide[j, c, a, pl.ds(r0, 8), :] = x

        pack(j, write)
        return 0

    lax.fori_loop(1, sections, pack_piece, 0)

    def write_own(c, a, r0, x):
        start[me, c, a, pl.ds(pl.multiple_of(top + r0, 8), 8), :] = x

    pack(me, write_own)
    pl.semaphore_wait(barrier, sections + bands - 2)

    for n in range(1, sections - 1):
        piece(turn(n), me).start()

    up_ok, down_ok = band > 0, band < bands - 1

    def to_above(s):
        return pltpu.make_async_remote_copy(
            src_ref=start.at[s, :, :, pl.ds(top, HALO), :],
            dst_ref=start.at[s, :, :, pl.ds(low, HALO), :],
            send_sem=halo_s.at[0, s], recv_sem=halo_r.at[0, s],
            device_id={"lat": band - 1}, device_id_type=MESH,
        )

    def to_below(s):
        return pltpu.make_async_remote_copy(
            src_ref=start.at[s, :, :, pl.ds(low - HALO, HALO), :],
            dst_ref=start.at[s, :, :, pl.ds(0, HALO), :],
            send_sem=halo_s.at[1, s], recv_sem=halo_r.at[1, s],
            device_id={"lat": band + 1}, device_id_type=MESH,
        )

    def st_above():
        return pltpu.make_async_remote_copy(
            src_ref=st.at[:, :, pl.ds(top, HALO), :], dst_ref=st.at[:, :, pl.ds(low, HALO), :],
            send_sem=st_s.at[0], recv_sem=st_r.at[0],
            device_id={"lat": band - 1}, device_id_type=MESH,
        )

    def st_below():
        return pltpu.make_async_remote_copy(
            src_ref=st.at[:, :, pl.ds(low - HALO, HALO), :], dst_ref=st.at[:, :, pl.ds(0, HALO), :],
            send_sem=st_s.at[1], recv_sem=st_r.at[1],
            device_id={"lat": band + 1}, device_id_type=MESH,
        )

    def send_halo(s):
        @pl.when(up_ok)
        def _():
            to_above(s).start()

        @pl.when(down_ok)
        def _():
            to_below(s).start()

    def recv_halo(s):
        @pl.when(down_ok)
        def _():
            to_above(s).wait_recv()

        @pl.when(up_ok)
        def _():
            to_below(s).wait_recv()

    send_halo(me)

    for n, (src, dst) in enumerate(singles):
        pltpu.make_async_copy(dst, dst, load_sem.at[1 + n]).wait()

    def prepare(r, _):
        r0 = pl.multiple_of(8 * r, 8)
        at, to = pl.ds(r0, 8), pl.ds(pl.multiple_of(top + r0, 8), 8)
        for c in range(wins):
            def window(ref):
                x = ref[at, c * 128 : c * 128 + 128]
                if c == per:
                    x = jnp.where(early, x, ref[at, c * 128 + 128 : c * 128 + 256])
                return x.astype(jnp.float32)

            sea = window(plain_mask)
            st[0, c, to, :] = window(plain_st.at[0]) * sea
            st[1, c, to, :] = sea
            st[2, c, to, :] = window(plain_st.at[1])
            st[3, c, to, :] = window(plain_st.at[2])
        return 0

    lax.fori_loop(0, rows // 8, prepare, 0)

    @pl.when(up_ok)
    def _():
        st_above().start()

    @pl.when(down_ok)
    def _():
        st_below().start()

    zero = jnp.zeros((8, 128), jnp.float32)

    def blank(first):
        def body(r, _):
            at = pl.ds(pl.multiple_of(first + 8 * r, 8), 8)
            for c in range(wins):
                for a in range(4):
                    st[a, c, at, :] = zero
                for s in range(sections):
                    for a in range(3):
                        start[s, c, a, at, :] = zero
            return 0

        lax.fori_loop(0, HALO // 8, body, 0)

    @pl.when(band == 0)
    def _():
        blank(0)

    @pl.when(band == bands - 1)
    def _():
        blank(low)

    def edge(lo, hi):
        for buf in (raised, flux):
            for c in range(wins):
                buf[c, pl.ds(8 * lo, 8), :] = zero
                buf[c, pl.ds(8 * hi + 8, 8), :] = zero

    acc[...] = jnp.zeros_like(acc)
    pltpu.make_async_copy(table, rows_in, load_sem.at[5]).wait()

    @pl.when(down_ok)
    def _():
        st_above().wait_recv()

    @pl.when(up_ok)
    def _():
        st_below().wait_recv()

    def lon_diff(xs, c):
        lane = lax.broadcasted_iota(jnp.int32, xs[c].shape, 1)
        after, before = xs[(c + 1) % wins], xs[c - 1]
        east_of = pltpu.roll(jnp.where(lane == 0, after, xs[c]), 127, 1)
        return east_of - pltpu.roll(jnp.where(lane == 127, before, xs[c]), 1, 1)

    def lon_diffs(xs):
        return [lon_diff(xs, c) for c in range(wins)]

    def lat_diff(ref, c, r0, high):
        return ref[c, pl.ds(r0 + 9, high), :] - ref[c, pl.ds(r0 + 7, high), :]

    def sweep(lo, hi, body):
        n = -(-(hi - lo) // STRIPS)
        size, more = divmod(hi - lo, n)
        at = lo
        for length, times in ((size + 1, more), (size, n - more)):
            if times:
                def turns(i, _, at=at, length=length):
                    r0 = pl.multiple_of(8 * (at + i * length), 8)
                    body(r0, 8 * length, pl.ds(r0, 8 * length), pl.ds(pl.multiple_of(r0 + 8, 8), 8 * length))
                    return 0

                lax.fori_loop(0, times, turns, 0)
                at += length * times

    def strip_sum(xs):
        return jnp.sum(sum(xs).reshape(-1, 8, 128), axis=0)

    def run(kind, source, s, lo, hi, finish, target_of=None):
        def push(h, c, at, step):
            if kind != "forced":
                return 0.5 * h
            base = 2 * (s * STEPS + step)
            return 0.5 * (h + (trig[base] * st[2, c, at, :] + trig[base + 1] * st[3, c, at, :]))

        def begin(r0, high_rows, at, padded):
            for c in range(wins):
                raised[c, padded, :] = push(source[s, c, 0, at, :], c, at, 0)

        sweep(lo, hi, begin)
        edge(lo, hi)

        def advance(step, is_first, is_last):
            def first(r0, high_rows, at, padded):
                slopes = lon_diffs([raised[c, padded, :] for c in range(wins)])
                cor = rows_in[0, at, :]
                for c in range(wins):
                    wet, sea = st[0, c, at, :], st[1, c, at, :]
                    dx, dy = slopes[c], lat_diff(raised, c, r0, high_rows)
                    if is_first:
                        u, v = source[s, c, 1, at, :], source[s, c, 2, at, :]
                    else:
                        u, v = east[c, at, :], north[c, at, :]
                    if kind == "back":
                        e = sea * (u + wet * dx)
                        f = sea * (v + wet * dy)
                        east[c, at, :] = DRAG_RATE * e - cor * f
                        north[c, at, :] = cor * e + DRAG_RATE * f
                        fluy[c, at, :], flux[c, padded, :] = 0.5 * e, 0.5 * f
                    else:
                        e = sea * (DRAG_RATE * u + cor * v - dx)
                        f = sea * (DRAG_RATE * v - cor * u - dy)
                        half = 0.5 * wet
                        east[c, at, :], north[c, at, :] = e, f
                        fluy[c, at, :], flux[c, padded, :] = half * e, half * f

            sweep(lo, hi, first)

            def second(r0, high_rows, at, padded):
                slopes = lon_diffs([fluy[c, at, :] for c in range(wins)])
                inside = rows_in[1, at, :]
                sums = []
                for c in range(wins):
                    d = slopes[c] + lat_diff(flux, c, r0, high_rows)
                    h = source[s, c, 0, at, :] if is_first else high[c, at, :]
                    h = (h + d if kind == "back" else h - d) * inside
                    if not is_last:
                        high[c, at, :], raised[c, padded, :] = h, push(h, c, at, step + 1)
                        continue
                    values = finish(c, at, (h, east[c, at, :], north[c, at, :]))
                    if kind == "free":
                        if c < per:
                            sums.append(values)
                    else:
                        target, slot = target_of
                        for a in range(3):
                            target[slot, c, a, at, :] = values[a]
                if sums:
                    acc[0] += strip_sum([x for x, _ in sums])
                    acc[1] += strip_sum([x for _, x in sums])

            inner = 1 if is_last else 0
            sweep(lo + inner, hi - inner, second)

        advance(0, True, False)

        def middle(step, _):
            advance(step, False, False)
            return 0

        lax.fori_loop(1, STEPS - 1, middle, 0)
        advance(STEPS - 1, False, True)

    def keep(c, at, values):
        return values

    def arrive(n):
        s = turn(n)
        piece(s, s).wait_recv()
        send_halo(s)

    def subtract(s, first_strip, last_strip):
        after = lax.rem(s + 1, sections)
        at = pl.ds(8 * first_strip, 8 * (last_strip - first_strip))

        def body(c, _):
            for a in range(3):
                mis[s, c, a, at, :] = mis[s, c, a, at, :] - start[after, c, a, at, :]
            return 0

        lax.fori_loop(0, wins, body, 0)

    columns = pl.ds(me * per, per)

    def give(source, target, send, recv, s, at_columns, slot):
        return pltpu.make_async_remote_copy(
            src_ref=source.at[s, pl.ds(0, per), :, pl.ds(top, rows), :],
            dst_ref=target.at[at_columns],
            send_sem=send.at[s], recv_sem=recv.at[slot],
            device_id={"sec": s}, device_id_type=MESH,
        )

    def send_mismatch(n):
        subtract(turn(n), top // 8, low // 8)
        give(mis, home, s2, r2, turn(n), columns, me).start()

    even = lax.rem(me, 2) == 0

    def forced(n, _):
        @pl.when(n == 1)
        def _():
            for i in range(1, sections - 1):
                arrive(i)
            for i in range(1, sections - 1):
                piece(turn(i), me).wait_send()
            piece(turn(sections - 1), me).start()

        s = turn(n)
        recv_halo(s)
        run("forced", start, s, 0, strips, keep, (mis, s))

        late = jnp.logical_and(n == sections - 2, even)

        @pl.when(jnp.logical_and(n > 0, jnp.logical_not(late)))
        def _():
            send_mismatch(n)

        @pl.when(n == sections - 2)
        def _():
            arrive(sections - 1)

        @pl.when(late)
        def _():
            send_mismatch(n)

        return 0

    lax.fori_loop(0, sections, forced, 0)
    subtract(me, top // 8, low // 8)
    own_mis = pltpu.make_async_copy(
        mis.at[me, pl.ds(0, per), :, pl.ds(top, rows), :],
        home.at[columns],
        own_sem.at[1],
    )
    own_mis.start()

    def fringe(s, _):
        subtract(s, 1, top // 8)
        subtract(s, low // 8, strips - 1)
        return 0

    lax.fori_loop(0, sections, fringe, 0)

    def back(i, _):
        s = turn(lax.rem(i, sections))
        before = lax.rem(s + sections - 1, sections)

        def done(c, at, values):
            return [x - mis[before, c, a, at, :] for a, x in enumerate(values)]

        run("back", mis, s, 1, strips - 1, done, (grad, s))

        @pl.when(i < sections)
        def _():
            give(grad, full, s3, r3, s, columns, me).start()

        return 0

    lax.fori_loop(1, sections + 1, back, 0)
    own_grad = pltpu.make_async_copy(
        grad.at[me, pl.ds(0, per), :, pl.ds(top, rows), :],
        full.at[columns],
        own_sem.at[2],
    )
    own_grad.start()

    def image(i, _):
        s = peer(i)
        after = peer(i + 1)

        def squares(c, at, values):
            pairs = [(x, grad[after, c, a, at, :]) for a, x in enumerate(values)]
            return sum(g * g for _, g in pairs), sum((x - g) * (x - g) for x, g in pairs)

        run("free", grad, s, 2, strips - 2, squares)
        return 0

    lax.fori_loop(0, sections, image, 0)

    total[band] = acc[...]

    def share_total(j, slot):
        return pltpu.make_async_remote_copy(
            src_ref=acc, dst_ref=total.at[slot], send_sem=ts.at[j], recv_sem=tr.at[slot],
            device_id={"lat": j}, device_id_type=MESH,
        )

    for i in range(1, bands):
        share_total(lax.rem(band + i, bands), band).start()
    for i in range(1, bands):
        j = lax.rem(band + i, bands)
        share_total(j, j).wait_recv()
    for i in range(1, bands):
        share_total(lax.rem(band + i, bands), band).wait_send()
    summed = total[0]
    for s in range(1, bands):
        summed = summed + total[s]
    acc[...] = summed
    part[me] = summed

    def share_part(j, slot):
        return pltpu.make_async_remote_copy(
            src_ref=acc, dst_ref=part.at[slot], send_sem=ps.at[j], recv_sem=pr.at[slot],
            device_id={"sec": j}, device_id_type=MESH,
        )

    for i in range(1, sections):
        share_part(peer(i), me).start()

    def rest(n, _):
        give(grad, full, s3, r3, turn(n), columns, me).start()
        return 0

    for i in range(1, sections):
        share_part(peer(i), peer(i)).wait_recv()
    summed = part[0]
    for s in range(1, sections):
        summed = summed + part[s]
    sums = jnp.sum(jnp.sum(summed, axis=2, keepdims=True), axis=1, keepdims=True)
    step = sums[0] / count / (sums[1] / count + EPSILON)
    step_out[...] = jnp.broadcast_to(step, (8, 128))

    own_mis.wait()

    def mismatches(i, _):
        s = peer(i)
        give(mis, home, s2, r2, s, columns, s).wait()
        return 0

    lax.fori_loop(1, sections, mismatches, 0)

    own_grad.wait()

    def grads(i, _):
        s = peer(i)
        give(grad, full, s3, r3, s, columns, s).wait_recv()
        return 0

    lax.fori_loop(1, sections, grads, 0)


    piece(turn(sections - 1), me).wait_send()

    def drain(i, _):
        s = peer(i)
        give(grad, full, s3, r3, s, columns, me).wait_send()
        return 0

    lax.fori_loop(1, sections, drain, 0)

    def drain_halo(i, _):
        s = peer(i)

        @pl.when(up_ok)
        def _():
            to_above(s).wait_send()

        @pl.when(down_ok)
        def _():
            to_below(s).wait_send()

        return 0

    lax.fori_loop(0, sections, drain_halo, 0)

    @pl.when(up_ok)
    def _():
        st_above().wait_send()

    @pl.when(down_ok)
    def _():
        st_below().wait_send()

    for i in range(1, sections):
        share_part(peer(i), me).wait_send()


def finish_kernel(fields, home, full, step, new_fields, mismatch, step_out):
    rows, width = fields.shape[1:]
    length = step[0:1, :]
    step_out[0, 0] = step[0, 0]

    def body(r, _):
        at = pl.ds(pl.multiple_of(8 * r, 8), 8)
        for c in range(width // 128):
            cols = slice(c * 128, c * 128 + 128)
            for a in range(3):
                new_fields[a, at, cols] = fields[a, at, cols] - length * full[c, a, at, :]
                mismatch[a, at, cols] = home[c, a, at, :]
        return 0

    lax.fori_loop(0, rows // 8, body, 0)


def shards(states, depth_field, land_mask, tide_cos, tide_sin):
    fields = states[0]
    rows, lon = fields.shape[1:]
    sections, bands = lax.axis_size("sec"), lax.axis_size("lat")
    share = lon // sections
    tall = rows + 2 * HALO
    lat_total = rows * bands
    ids = np.arange(lat_total + 2 * HALO, dtype=np.float32) - HALO
    inside = ((ids >= 0) & (ids < lat_total)).astype(np.float32)
    turned = np.float32(math.pi) * (ids + np.float32(0.5)) / np.float32(lat_total)
    coriolis = np.float32(CORIOLIS_MAX) * np.sin(turned - np.float32(0.5 * math.pi))
    row_table = np.broadcast_to(np.stack([coriolis, inside])[:, :, None], (2, ids.size, 128))
    row_table = jnp.asarray(row_table.astype(np.float32))
    angles = np.float32(TWO_PI) * np.arange(sections * STEPS, dtype=np.float32) / np.float32(
        sections * STEPS
    )
    trig = jnp.asarray(np.stack([np.cos(angles), np.sin(angles)], axis=1).reshape(-1))
    f32 = jnp.float32
    dma = pltpu.SemaphoreType.DMA
    any_spec = pl.BlockSpec(memory_space=pl.ANY)
    vmem = pl.BlockSpec(memory_space=pltpu.VMEM)
    tiles, wins = lon // 128, share // 128 + 1
    stacked = pltpu.VMEM((sections, wins, 3, tall, 128), f32)
    plain = pltpu.VMEM((wins, tall, 128), f32)
    padded = pltpu.VMEM((wins, tall + 16, 128), f32)
    gathered = jax.ShapeDtypeStruct((tiles, 3, rows, 128), f32)
    home, full, step = pl.pallas_call(
        functools.partial(kernel, sections, bands, float(sections * 3 * lat_total * lon)),
        out_shape=(
            gathered,
            gathered,
            jax.ShapeDtypeStruct((8, 128), f32),
        ),
        in_specs=[any_spec] * 6 + [pl.BlockSpec(memory_space=pltpu.SMEM)],
        out_specs=(any_spec, any_spec, vmem),
        scratch_shapes=[
            pltpu.VMEM((3, rows, lon), f32),
            pltpu.VMEM((3, rows, share + 256), f32),
            pltpu.VMEM((rows, share + 256), jnp.int32),
            pltpu.VMEM((2, tall, 128), f32),
            pltpu.VMEM((sections, wins, 3, rows, 128), f32),
            pltpu.VMEM((4, wins, tall, 128), f32),
            stacked, stacked, stacked,
            plain, plain, plain, padded, padded, plain,
            pltpu.VMEM((2, 8, 128), f32),
            pltpu.VMEM((sections, 2, 8, 128), f32),
            pltpu.VMEM((bands, 2, 8, 128), f32),
            dma((6,)),
            dma((sections,)), dma((sections,)),
            dma((2, sections)), dma((2, sections)),
            dma((2,)), dma((2,)),
            dma((sections,)), dma((sections,)),
            dma((sections,)), dma((sections,)),
            dma((3,)),
            dma((sections,)), dma((sections,)),
            dma((bands,)), dma((bands,)),
        ],
        compiler_params=pltpu.CompilerParams(
            collective_id=0, has_side_effects=True, vmem_limit_bytes=60 * 1024 * 1024
        ),
        name="shooting",
    )(fields, depth_field, land_mask, tide_cos, tide_sin, row_table, trig)
    half = 2 * share
    block = pl.BlockSpec((3, rows, half), lambda i: (0, 0, i))
    by_tile = pl.BlockSpec((half // 128, 3, rows, 128), lambda i: (i, 0, 0, 0))
    new_fields, mismatch, length = pl.pallas_call(
        finish_kernel,
        grid=(sections // 2,),
        out_shape=(jax.ShapeDtypeStruct(fields.shape, f32),) * 2 + (jax.ShapeDtypeStruct((1, 1), f32),),
        in_specs=[block, by_tile, by_tile, pl.BlockSpec((8, 128), lambda i: (0, 0))],
        out_specs=(block, block, pl.BlockSpec(memory_space=pltpu.SMEM)),
        compiler_params=pltpu.CompilerParams(vmem_limit_bytes=60 * 1024 * 1024),
        name="update",
    )(fields, home, full, step)
    return new_fields[None], mismatch[None], length.reshape(())


def solution(mesh):
    return jax.shard_map(
        shards,
        mesh=mesh,
        in_specs=(
            P("sec", None, "lat", None),
            P("lat", None),
            P("lat", None),
            P("lat", None),
            P("lat", None),
        ),
        out_specs=(P("sec", None, "lat", None), P("sec", None, "lat", None), P()),
        check_vma=False,
    )
```

```python
import functools
import math

import jax
import jax.numpy as jnp
import numpy as np
from jax import lax
from jax.experimental import pallas as pl
from jax.experimental.pallas import tpu as pltpu
from jax.sharding import PartitionSpec as P

STEPS = 4
DRAG_RATE = 0.9
CORIOLIS_MAX = 0.3
EPSILON = 1e-06
TWO_PI = 2.0 * math.pi
HALO = 24
STRIPS = 7
MESH = pl.DeviceIdType.MESH


def kernel(
    sections, bands, count,
    states, depth, mask, tide_one, tide_two, row_table, trig,
    home, full, step_out,
    plain, plain_st, plain_mask, rows_in, wide, st, start, mis, grad,
    high, east, north, raised, flux, fluy, acc, part, total,
    load_sem, s1, r1, halo_s, halo_r, st_s, st_r, s2, r2, s3, r3, own_sem, ps, pr, ts, tr,
):
    me = lax.axis_index("sec")
    band = lax.axis_index("lat")
    rows, lon = states.shape[1], states.shape[2]
    share = lon // sections
    per, tiles = share // 128, lon // 128
    wins = per + 1
    tall = rows + 2 * HALO
    strips = tall // 8
    top, low = HALO, HALO + rows

    def peer(i):
        return lax.rem(me + i, sections)

    def tile(c):
        return pl.ds(pl.multiple_of(c * 128, 128), 128)

    barrier = pltpu.get_barrier_semaphore()
    for i in range(1, sections):
        pl.semaphore_signal(barrier, inc=1, device_id={"sec": peer(i)}, device_id_type=MESH)
    for i in range(1, bands):
        pl.semaphore_signal(
            barrier, inc=1, device_id={"lat": lax.rem(band + i, bands)}, device_id_type=MESH
        )
    pltpu.make_async_copy(states, plain, load_sem.at[0]).start()
    singles = (
        (depth, plain_st.at[0]), (mask, plain_mask), (tide_one, plain_st.at[1]), (tide_two, plain_st.at[2])
    )
    ends = (
        (pl.ds(pl.multiple_of(me * share, 128), share), pl.ds(0, share)),
        (tile(lax.rem(me * per + per, tiles)), pl.ds(share, 128)),
        (tile(lax.rem(me * per + tiles - 1, tiles)), pl.ds(share + 128, 128)),
    )
    for n, (src, dst) in enumerate(singles):
        for there, here in ends:
            pltpu.make_async_copy(src.at[:, there], dst.at[:, here], load_sem.at[1 + n]).start()
    table = row_table.at[:, pl.ds(pl.multiple_of(band * rows, 8), tall), :]
    pltpu.make_async_copy(table, rows_in, load_sem.at[5]).start()

    pltpu.make_async_copy(states, plain, load_sem.at[0]).wait()
    early = lax.broadcasted_iota(jnp.int32, (8, 128), 1) < 64

    def pack(j, write):
        def body(r, _):
            r0 = pl.multiple_of(8 * r, 8)
            at = pl.ds(r0, 8)
            for a in range(3):
                for c in range(per):
                    write(c, a, r0, plain[a, at, tile(j * per + c)])
                after = plain[a, at, tile(lax.rem(j * per + per, tiles))]
                before = plain[a, at, tile(lax.rem(j * per + tiles - 1, tiles))]
                write(per, a, r0, jnp.where(early, after, before))
            return 0

        lax.fori_loop(0, rows // 8, body, 0)

    def piece(j, slot):
        return pltpu.make_async_remote_copy(
            src_ref=wide.at[j],
            dst_ref=start.at[me, :, :, pl.ds(top, rows), :],
            send_sem=s1.at[j],
            recv_sem=r1.at[slot],
            device_id={"sec": j},
            device_id_type=MESH,
        )

    def turn(n):
        return lax.rem(me + jnp.where(lax.rem(me, 2) == 0, n, sections - n), sections)

    def pack_piece(n, _):
        j = turn(n)

        def write(c, a, r0, x):
            wide[j, c, a, pl.ds(r0, 8), :] = x

        pack(j, write)
        return 0

    lax.fori_loop(1, sections, pack_piece, 0)

    def write_own(c, a, r0, x):
        start[me, c, a, pl.ds(pl.multiple_of(top + r0, 8), 8), :] = x

    pack(me, write_own)
    pl.semaphore_wait(barrier, sections + bands - 2)

    for n in range(1, sections):
        piece(turn(n), me).start()

    up_ok, down_ok = band > 0, band < bands - 1

    def to_above(s):
        return pltpu.make_async_remote_copy(
            src_ref=start.at[s, :, :, pl.ds(top, HALO), :],
            dst_ref=start.at[s, :, :, pl.ds(low, HALO), :],
            send_sem=halo_s.at[0, s], recv_sem=halo_r.at[0, s],
            device_id={"lat": band - 1}, device_id_type=MESH,
        )

    def to_below(s):
        return pltpu.make_async_remote_copy(
            src_ref=start.at[s, :, :, pl.ds(low - HALO, HALO), :],
            dst_ref=start.at[s, :, :, pl.ds(0, HALO), :],
            send_sem=halo_s.at[1, s], recv_sem=halo_r.at[1, s],
            device_id={"lat": band + 1}, device_id_type=MESH,
        )

    def st_above():
        return pltpu.make_async_remote_copy(
            src_ref=st.at[:, :, pl.ds(top, HALO), :], dst_ref=st.at[:, :, pl.ds(low, HALO), :],
            send_sem=st_s.at[0], recv_sem=st_r.at[0],
            device_id={"lat": band - 1}, device_id_type=MESH,
        )

    def st_below():
        return pltpu.make_async_remote_copy(
            src_ref=st.at[:, :, pl.ds(low - HALO, HALO), :], dst_ref=st.at[:, :, pl.ds(0, HALO), :],
            send_sem=st_s.at[1], recv_sem=st_r.at[1],
            device_id={"lat": band + 1}, device_id_type=MESH,
        )

    def send_halo(s):
        @pl.when(up_ok)
        def _():
            to_above(s).start()

        @pl.when(down_ok)
        def _():
            to_below(s).start()

    def recv_halo(s):
        @pl.when(down_ok)
        def _():
            to_above(s).wait_recv()

        @pl.when(up_ok)
        def _():
            to_below(s).wait_recv()

    send_halo(me)

    for n, (src, dst) in enumerate(singles):
        pltpu.make_async_copy(dst, dst, load_sem.at[1 + n]).wait()

    def prepare(r, _):
        r0 = pl.multiple_of(8 * r, 8)
        at, to = pl.ds(r0, 8), pl.ds(pl.multiple_of(top + r0, 8), 8)
        for c in range(wins):
            def window(ref):
                x = ref[at, c * 128 : c * 128 + 128]
                if c == per:
                    x = jnp.where(early, x, ref[at, c * 128 + 128 : c * 128 + 256])
                return x.astype(jnp.float32)

            sea = window(plain_mask)
            st[0, c, to, :] = window(plain_st.at[0]) * sea
            st[1, c, to, :] = sea
            st[2, c, to, :] = window(plain_st.at[1])
            st[3, c, to, :] = window(plain_st.at[2])
        return 0

    lax.fori_loop(0, rows // 8, prepare, 0)

    @pl.when(up_ok)
    def _():
        st_above().start()

    @pl.when(down_ok)
    def _():
        st_below().start()

    zero = jnp.zeros((8, 128), jnp.float32)

    def blank(first):
        def body(r, _):
            at = pl.ds(pl.multiple_of(first + 8 * r, 8), 8)
            for c in range(wins):
                for a in range(4):
                    st[a, c, at, :] = zero
                for s in range(sections):
                    for a in range(3):
                        start[s, c, a, at, :] = zero
            return 0

        lax.fori_loop(0, HALO // 8, body, 0)

    @pl.when(band == 0)
    def _():
        blank(0)

    @pl.when(band == bands - 1)
    def _():
        blank(low)

    def edge(lo, hi):
        for buf in (raised, flux):
            for c in range(wins):
                buf[c, pl.ds(8 * lo, 8), :] = zero
                buf[c, pl.ds(8 * hi + 8, 8), :] = zero

    acc[...] = jnp.zeros_like(acc)
    pltpu.make_async_copy(table, rows_in, load_sem.at[5]).wait()

    @pl.when(down_ok)
    def _():
        st_above().wait_recv()

    @pl.when(up_ok)
    def _():
        st_below().wait_recv()

    def lon_diff(xs, c):
        lane = lax.broadcasted_iota(jnp.int32, xs[c].shape, 1)
        after, before = xs[(c + 1) % wins], xs[c - 1]
        east_of = pltpu.roll(jnp.where(lane == 0, after, xs[c]), 127, 1)
        return east_of - pltpu.roll(jnp.where(lane == 127, before, xs[c]), 1, 1)

    def lon_diffs(xs):
        return [lon_diff(xs, c) for c in range(wins)]

    def lat_diff(ref, c, r0, high):
        return ref[c, pl.ds(r0 + 9, high), :] - ref[c, pl.ds(r0 + 7, high), :]

    def sweep(lo, hi, body):
        n = -(-(hi - lo) // STRIPS)
        size, more = divmod(hi - lo, n)
        at = lo
        for length, times in ((size + 1, more), (size, n - more)):
            if times:
                def turns(i, _, at=at, length=length):
                    r0 = pl.multiple_of(8 * (at + i * length), 8)
                    body(r0, 8 * length, pl.ds(r0, 8 * length), pl.ds(pl.multiple_of(r0 + 8, 8), 8 * length))
                    return 0

                lax.fori_loop(0, times, turns, 0)
                at += length * times

    def strip_sum(xs):
        return jnp.sum(sum(xs).reshape(-1, 8, 128), axis=0)

    def run(kind, source, s, lo, hi, finish, target_of=None):
        def push(h, c, at, step):
            if kind != "forced":
                return 0.5 * h
            base = 2 * (s * STEPS + step)
            return 0.5 * (h + (trig[base] * st[2, c, at, :] + trig[base + 1] * st[3, c, at, :]))

        def begin(r0, high_rows, at, padded):
            for c in range(wins):
                raised[c, padded, :] = push(source[s, c, 0, at, :], c, at, 0)

        sweep(lo, hi, begin)
        edge(lo, hi)

        def advance(step, is_first, is_last):
            def first(r0, high_rows, at, padded):
                slopes = lon_diffs([raised[c, padded, :] for c in range(wins)])
                cor = rows_in[0, at, :]
                for c in range(wins):
                    wet, sea = st[0, c, at, :], st[1, c, at, :]
                    dx, dy = slopes[c], lat_diff(raised, c, r0, high_rows)
                    if is_first:
                        u, v = source[s, c, 1, at, :], source[s, c, 2, at, :]
                    else:
                        u, v = east[c, at, :], north[c, at, :]
                    if kind == "back":
                        e = sea * (u + wet * dx)
                        f = sea * (v + wet * dy)
                        east[c, at, :] = DRAG_RATE * e - cor * f
                        north[c, at, :] = cor * e + DRAG_RATE * f
                        fluy[c, at, :], flux[c, padded, :] = 0.5 * e, 0.5 * f
                    else:
                        e = sea * (DRAG_RATE * u + cor * v - dx)
                        f = sea * (DRAG_RATE * v - cor * u - dy)
                        half = 0.5 * wet
                        east[c, at, :], north[c, at, :] = e, f
                        fluy[c, at, :], flux[c, padded, :] = half * e, half * f

            sweep(lo, hi, first)

            def second(r0, high_rows, at, padded):
                slopes = lon_diffs([fluy[c, at, :] for c in range(wins)])
                inside = rows_in[1, at, :]
                sums = []
                for c in range(wins):
                    d = slopes[c] + lat_diff(flux, c, r0, high_rows)
                    h = source[s, c, 0, at, :] if is_first else high[c, at, :]
                    h = (h + d if kind == "back" else h - d) * inside
                    if not is_last:
                        high[c, at, :], raised[c, padded, :] = h, push(h, c, at, step + 1)
                        continue
                    values = finish(c, at, (h, east[c, at, :], north[c, at, :]))
                    if kind == "free":
                        if c < per:
                            sums.append(values)
                    else:
                        target, slot = target_of
                        for a in range(3):
                            target[slot, c, a, at, :] = values[a]
                if sums:
                    acc[0] += strip_sum([x for x, _ in sums])
                    acc[1] += strip_sum([x for _, x in sums])

            inner = 1 if is_last else 0
            sweep(lo + inner, hi - inner, second)

        advance(0, True, False)

        def middle(step, _):
            advance(step, False, False)
            return 0

        lax.fori_loop(1, STEPS - 1, middle, 0)
        advance(STEPS - 1, False, True)

    def keep(c, at, values):
        return values

    def arrive(n):
        s = turn(n)
        piece(s, s).wait_recv()
        send_halo(s)

    def subtract(s, first_strip, last_strip):
        after = lax.rem(s + 1, sections)
        at = pl.ds(8 * first_strip, 8 * (last_strip - first_strip))

        def body(c, _):
            for a in range(3):
                mis[s, c, a, at, :] = mis[s, c, a, at, :] - start[after, c, a, at, :]
            return 0

        lax.fori_loop(0, wins, body, 0)

    columns = pl.ds(me * per, per)

    def give(source, target, send, recv, s, at_columns, slot):
        return pltpu.make_async_remote_copy(
            src_ref=source.at[s, pl.ds(0, per), :, pl.ds(top, rows), :],
            dst_ref=target.at[at_columns],
            send_sem=send.at[s], recv_sem=recv.at[slot],
            device_id={"sec": s}, device_id_type=MESH,
        )

    def send_mismatch(n):
        subtract(turn(n), top // 8, low // 8)
        give(mis, home, s2, r2, turn(n), columns, me).start()

    even = lax.rem(me, 2) == 0

    def forced(n, _):
        @pl.when(n == 1)
        def _():
            for i in range(1, sections - 1):
                arrive(i)
            for i in range(1, sections - 1):
                piece(turn(i), me).wait_send()

        s = turn(n)
        recv_halo(s)
        run("forced", start, s, 0, strips, keep, (mis, s))

        late = jnp.logical_and(n == sections - 2, even)

        @pl.when(jnp.logical_and(n > 0, jnp.logical_not(late)))
        def _():
            send_mismatch(n)

        @pl.when(n == sections - 2)
        def _():
            arrive(sections - 1)

        @pl.when(late)
        def _():
            send_mismatch(n)

        return 0

    lax.fori_loop(0, sections, forced, 0)
    subtract(me, top // 8, low // 8)
    own_mis = pltpu.make_async_copy(
        mis.at[me, pl.ds(0, per), :, pl.ds(top, rows), :],
        home.at[columns],
        own_sem.at[1],
    )
    own_mis.start()

    def fringe(s, _):
        subtract(s, 1, top // 8)
        subtract(s, low // 8, strips - 1)
        return 0

    lax.fori_loop(0, sections, fringe, 0)

    def back(i, _):
        s = turn(lax.rem(i, sections))
        before = lax.rem(s + sections - 1, sections)

        def done(c, at, values):
            return [x - mis[before, c, a, at, :] for a, x in enumerate(values)]

        run("back", mis, s, 1, strips - 1, done, (grad, s))

        @pl.when(i < sections)
        def _():
            give(grad, full, s3, r3, s, columns, me).start()

        return 0

    lax.fori_loop(1, sections + 1, back, 0)
    own_grad = pltpu.make_async_copy(
        grad.at[me, pl.ds(0, per), :, pl.ds(top, rows), :],
        full.at[columns],
        own_sem.at[2],
    )
    own_grad.start()

    def image(i, _):
        s = peer(i)
        after = peer(i + 1)

        def squares(c, at, values):
            pairs = [(x, grad[after, c, a, at, :]) for a, x in enumerate(values)]
            return sum(g * g for _, g in pairs), sum((x - g) * (x - g) for x, g in pairs)

        run("free", grad, s, 2, strips - 2, squares)
        return 0

    lax.fori_loop(0, sections, image, 0)

    total[band] = acc[...]

    def share_total(j, slot):
        return pltpu.make_async_remote_copy(
            src_ref=acc, dst_ref=total.at[slot], send_sem=ts.at[j], recv_sem=tr.at[slot],
            device_id={"lat": j}, device_id_type=MESH,
        )

    for i in range(1, bands):
        share_total(lax.rem(band + i, bands), band).start()
    for i in range(1, bands):
        j = lax.rem(band + i, bands)
        share_total(j, j).wait_recv()
    for i in range(1, bands):
        share_total(lax.rem(band + i, bands), band).wait_send()
    summed = total[0]
    for s in range(1, bands):
        summed = summed + total[s]
    acc[...] = summed
    part[me] = summed

    def share_part(j, slot):
        return pltpu.make_async_remote_copy(
            src_ref=acc, dst_ref=part.at[slot], send_sem=ps.at[j], recv_sem=pr.at[slot],
            device_id={"sec": j}, device_id_type=MESH,
        )

    for i in range(1, sections):
        share_part(peer(i), me).start()

    def rest(n, _):
        give(grad, full, s3, r3, turn(n), columns, me).start()
        return 0

    for i in range(1, sections):
        share_part(peer(i), peer(i)).wait_recv()
    summed = part[0]
    for s in range(1, sections):
        summed = summed + part[s]
    sums = jnp.sum(jnp.sum(summed, axis=2, keepdims=True), axis=1, keepdims=True)
    step = sums[0] / count / (sums[1] / count + EPSILON)
    step_out[...] = jnp.broadcast_to(step, (8, 128))

    own_mis.wait()

    def mismatches(i, _):
        s = peer(i)
        give(mis, home, s2, r2, s, columns, s).wait()
        return 0

    lax.fori_loop(1, sections, mismatches, 0)

    own_grad.wait()

    def grads(i, _):
        s = peer(i)
        give(grad, full, s3, r3, s, columns, s).wait_recv()
        return 0

    lax.fori_loop(1, sections, grads, 0)


    piece(turn(sections - 1), me).wait_send()

    def drain(i, _):
        s = peer(i)
        give(grad, full, s3, r3, s, columns, me).wait_send()
        return 0

    lax.fori_loop(1, sections, drain, 0)

    def drain_halo(i, _):
        s = peer(i)

        @pl.when(up_ok)
        def _():
            to_above(s).wait_send()

        @pl.when(down_ok)
        def _():
            to_below(s).wait_send()

        return 0

    lax.fori_loop(0, sections, drain_halo, 0)

    @pl.when(up_ok)
    def _():
        st_above().wait_send()

    @pl.when(down_ok)
    def _():
        st_below().wait_send()

    for i in range(1, sections):
        share_part(peer(i), me).wait_send()


def finish_kernel(fields, home, full, step, new_fields, mismatch, step_out):
    rows, width = fields.shape[1:]
    length = step[0:1, :]
    step_out[0, 0] = step[0, 0]

    def body(r, _):
        at = pl.ds(pl.multiple_of(8 * r, 8), 8)
        for c in range(width // 128):
            cols = slice(c * 128, c * 128 + 128)
            for a in range(3):
                new_fields[a, at, cols] = fields[a, at, cols] - length * full[c, a, at, :]
                mismatch[a, at, cols] = home[c, a, at, :]
        return 0

    lax.fori_loop(0, rows // 8, body, 0)


def shards(states, depth_field, land_mask, tide_cos, tide_sin):
    fields = states[0]
    rows, lon = fields.shape[1:]
    sections, bands = lax.axis_size("sec"), lax.axis_size("lat")
    share = lon // sections
    tall = rows + 2 * HALO
    lat_total = rows * bands
    ids = np.arange(lat_total + 2 * HALO, dtype=np.float32) - HALO
    inside = ((ids >= 0) & (ids < lat_total)).astype(np.float32)
    turned = np.float32(math.pi) * (ids + np.float32(0.5)) / np.float32(lat_total)
    coriolis = np.float32(CORIOLIS_MAX) * np.sin(turned - np.float32(0.5 * math.pi))
    row_table = np.broadcast_to(np.stack([coriolis, inside])[:, :, None], (2, ids.size, 128))
    row_table = jnp.asarray(row_table.astype(np.float32))
    angles = np.float32(TWO_PI) * np.arange(sections * STEPS, dtype=np.float32) / np.float32(
        sections * STEPS
    )
    trig = jnp.asarray(np.stack([np.cos(angles), np.sin(angles)], axis=1).reshape(-1))
    f32 = jnp.float32
    dma = pltpu.SemaphoreType.DMA
    any_spec = pl.BlockSpec(memory_space=pl.ANY)
    vmem = pl.BlockSpec(memory_space=pltpu.VMEM)
    tiles, wins = lon // 128, share // 128 + 1
    stacked = pltpu.VMEM((sections, wins, 3, tall, 128), f32)
    plain = pltpu.VMEM((wins, tall, 128), f32)
    padded = pltpu.VMEM((wins, tall + 16, 128), f32)
    gathered = jax.ShapeDtypeStruct((tiles, 3, rows, 128), f32)
    home, full, step = pl.pallas_call(
        functools.partial(kernel, sections, bands, float(sections * 3 * lat_total * lon)),
        out_shape=(
            gathered,
            gathered,
            jax.ShapeDtypeStruct((8, 128), f32),
        ),
        in_specs=[any_spec] * 6 + [pl.BlockSpec(memory_space=pltpu.SMEM)],
        out_specs=(any_spec, any_spec, vmem),
        scratch_shapes=[
            pltpu.VMEM((3, rows, lon), f32),
            pltpu.VMEM((3, rows, share + 256), f32),
            pltpu.VMEM((rows, share + 256), jnp.int32),
            pltpu.VMEM((2, tall, 128), f32),
            pltpu.VMEM((sections, wins, 3, rows, 128), f32),
            pltpu.VMEM((4, wins, tall, 128), f32),
            stacked, stacked, stacked,
            plain, plain, plain, padded, padded, plain,
            pltpu.VMEM((2, 8, 128), f32),
            pltpu.VMEM((sections, 2, 8, 128), f32),
            pltpu.VMEM((bands, 2, 8, 128), f32),
            dma((6,)),
            dma((sections,)), dma((sections,)),
            dma((2, sections)), dma((2, sections)),
            dma((2,)), dma((2,)),
            dma((sections,)), dma((sections,)),
            dma((sections,)), dma((sections,)),
            dma((3,)),
            dma((sections,)), dma((sections,)),
            dma((bands,)), dma((bands,)),
        ],
        compiler_params=pltpu.CompilerParams(
            collective_id=0, has_side_effects=True, vmem_limit_bytes=60 * 1024 * 1024
        ),
        name="shooting",
    )(fields, depth_field, land_mask, tide_cos, tide_sin, row_table, trig)
    half = 2 * share
    block = pl.BlockSpec((3, rows, half), lambda i: (0, 0, i))
    by_tile = pl.BlockSpec((half // 128, 3, rows, 128), lambda i: (i, 0, 0, 0))
    new_fields, mismatch, length = pl.pallas_call(
        finish_kernel,
        grid=(sections // 2,),
        out_shape=(jax.ShapeDtypeStruct(fields.shape, f32),) * 2 + (jax.ShapeDtypeStruct((1, 1), f32),),
        in_specs=[block, by_tile, by_tile, pl.BlockSpec((8, 128), lambda i: (0, 0))],
        out_specs=(block, block, pl.BlockSpec(memory_space=pltpu.SMEM)),
        compiler_params=pltpu.CompilerParams(vmem_limit_bytes=60 * 1024 * 1024),
        name="update",
    )(fields, home, full, step)
    return new_fields[None], mismatch[None], length.reshape(())


def solution(mesh):
    return jax.shard_map(
        shards,
        mesh=mesh,
        in_specs=(
            P("sec", None, "lat", None),
            P("lat", None),
            P("lat", None),
            P("lat", None),
            P("lat", None),
        ),
        out_specs=(P("sec", None, "lat", None), P("sec", None, "lat", None), P()),
        check_vma=False,
    )
```

```python
import functools
import math

import jax
import jax.numpy as jnp
import numpy as np
from jax import lax
from jax.experimental import pallas as pl
from jax.experimental.pallas import tpu as pltpu
from jax.sharding import PartitionSpec as P

STEPS = 4
DRAG_RATE = 0.9
CORIOLIS_MAX = 0.3
EPSILON = 1e-06
TWO_PI = 2.0 * math.pi
HALO = 24
STRIPS = 7
MESH = pl.DeviceIdType.MESH


def kernel(
    sections, bands, count,
    states, depth, mask, tide_one, tide_two, row_table, trig,
    home, full, step_out,
    plain, plain_st, plain_mask, rows_in, wide, st, start, mis, grad,
    high, east, north, raised, flux, fluy, acc, part, total,
    load_sem, s1, r1, halo_s, halo_r, st_s, st_r, s2, r2, s3, r3, own_sem, ps, pr, ts, tr,
):
    me = lax.axis_index("sec")
    band = lax.axis_index("lat")
    rows, lon = states.shape[1], states.shape[2]
    share = lon // sections
    per, tiles = share // 128, lon // 128
    wins = per + 1
    tall = rows + 2 * HALO
    strips = tall // 8
    top, low = HALO, HALO + rows

    def peer(i):
        return lax.rem(me + i, sections)

    def tile(c):
        return pl.ds(pl.multiple_of(c * 128, 128), 128)

    barrier = pltpu.get_barrier_semaphore()
    for i in range(1, sections):
        pl.semaphore_signal(barrier, inc=1, device_id={"sec": peer(i)}, device_id_type=MESH)
    for i in range(1, bands):
        pl.semaphore_signal(
            barrier, inc=1, device_id={"lat": lax.rem(band + i, bands)}, device_id_type=MESH
        )
    pltpu.make_async_copy(states, plain, load_sem.at[0]).start()
    singles = (
        (depth, plain_st.at[0]), (mask, plain_mask), (tide_one, plain_st.at[1]), (tide_two, plain_st.at[2])
    )
    ends = (
        (pl.ds(pl.multiple_of(me * share, 128), share), pl.ds(0, share)),
        (tile(lax.rem(me * per + per, tiles)), pl.ds(share, 128)),
        (tile(lax.rem(me * per + tiles - 1, tiles)), pl.ds(share + 128, 128)),
    )
    for n, (src, dst) in enumerate(singles):
        for there, here in ends:
            pltpu.make_async_copy(src.at[:, there], dst.at[:, here], load_sem.at[1 + n]).start()
    table = row_table.at[:, pl.ds(pl.multiple_of(band * rows, 8), tall), :]
    pltpu.make_async_copy(table, rows_in, load_sem.at[5]).start()

    pltpu.make_async_copy(states, plain, load_sem.at[0]).wait()
    early = lax.broadcasted_iota(jnp.int32, (8, 128), 1) < 64

    def pack(j, write):
        def body(r, _):
            r0 = pl.multiple_of(8 * r, 8)
            at = pl.ds(r0, 8)
            for a in range(3):
                for c in range(per):
                    write(c, a, r0, plain[a, at, tile(j * per + c)])
                after = plain[a, at, tile(lax.rem(j * per + per, tiles))]
                before = plain[a, at, tile(lax.rem(j * per + tiles - 1, tiles))]
                write(per, a, r0, jnp.where(early, after, before))
            return 0

        lax.fori_loop(0, rows // 8, body, 0)

    def piece(j, slot):
        return pltpu.make_async_remote_copy(
            src_ref=wide.at[j],
            dst_ref=start.at[me, :, :, pl.ds(top, rows), :],
            send_sem=s1.at[j],
            recv_sem=r1.at[slot],
            device_id={"sec": j},
            device_id_type=MESH,
        )

    def turn(n):
        return lax.rem(me + jnp.where(lax.rem(me, 2) == 0, n, sections - n), sections)

    def pack_piece(n, _):
        j = turn(n)

        def write(c, a, r0, x):
            wide[j, c, a, pl.ds(r0, 8), :] = x

        pack(j, write)
        return 0

    lax.fori_loop(1, sections, pack_piece, 0)

    def write_own(c, a, r0, x):
        start[me, c, a, pl.ds(pl.multiple_of(top + r0, 8), 8), :] = x

    pack(me, write_own)
    pl.semaphore_wait(barrier, sections + bands - 2)

    def order(n):
        return jnp.where(jnp.logical_and(lax.rem(band, 2) == 1, n < 3), 3 - n, n)

    for n in range(1, sections):
        piece(turn(order(n)), me).start()

    up_ok, down_ok = band > 0, band < bands - 1

    def to_above(s):
        return pltpu.make_async_remote_copy(
            src_ref=start.at[s, :, :, pl.ds(top, HALO), :],
            dst_ref=start.at[s, :, :, pl.ds(low, HALO), :],
            send_sem=halo_s.at[0, s], recv_sem=halo_r.at[0, s],
            device_id={"lat": band - 1}, device_id_type=MESH,
        )

    def to_below(s):
        return pltpu.make_async_remote_copy(
            src_ref=start.at[s, :, :, pl.ds(low - HALO, HALO), :],
            dst_ref=start.at[s, :, :, pl.ds(0, HALO), :],
            send_sem=halo_s.at[1, s], recv_sem=halo_r.at[1, s],
            device_id={"lat": band + 1}, device_id_type=MESH,
        )

    def st_above():
        return pltpu.make_async_remote_copy(
            src_ref=st.at[:, :, pl.ds(top, HALO), :], dst_ref=st.at[:, :, pl.ds(low, HALO), :],
            send_sem=st_s.at[0], recv_sem=st_r.at[0],
            device_id={"lat": band - 1}, device_id_type=MESH,
        )

    def st_below():
        return pltpu.make_async_remote_copy(
            src_ref=st.at[:, :, pl.ds(low - HALO, HALO), :], dst_ref=st.at[:, :, pl.ds(0, HALO), :],
            send_sem=st_s.at[1], recv_sem=st_r.at[1],
            device_id={"lat": band + 1}, device_id_type=MESH,
        )

    def send_halo(s):
        @pl.when(up_ok)
        def _():
            to_above(s).start()

        @pl.when(down_ok)
        def _():
            to_below(s).start()

    def recv_halo(s):
        @pl.when(down_ok)
        def _():
            to_above(s).wait_recv()

        @pl.when(up_ok)
        def _():
            to_below(s).wait_recv()

    send_halo(me)

    for n, (src, dst) in enumerate(singles):
        pltpu.make_async_copy(dst, dst, load_sem.at[1 + n]).wait()

    def prepare(r, _):
        r0 = pl.multiple_of(8 * r, 8)
        at, to = pl.ds(r0, 8), pl.ds(pl.multiple_of(top + r0, 8), 8)
        for c in range(wins):
            def window(ref):
                x = ref[at, c * 128 : c * 128 + 128]
                if c == per:
                    x = jnp.where(early, x, ref[at, c * 128 + 128 : c * 128 + 256])
                return x.astype(jnp.float32)

            sea = window(plain_mask)
            st[0, c, to, :] = window(plain_st.at[0]) * sea
            st[1, c, to, :] = sea
            st[2, c, to, :] = window(plain_st.at[1])
            st[3, c, to, :] = window(plain_st.at[2])
        return 0

    lax.fori_loop(0, rows // 8, prepare, 0)

    @pl.when(up_ok)
    def _():
        st_above().start()

    @pl.when(down_ok)
    def _():
        st_below().start()

    zero = jnp.zeros((8, 128), jnp.float32)

    def blank(first):
        def body(r, _):
            at = pl.ds(pl.multiple_of(first + 8 * r, 8), 8)
            for c in range(wins):
                for a in range(4):
                    st[a, c, at, :] = zero
                for s in range(sections):
                    for a in range(3):
                        start[s, c, a, at, :] = zero
            return 0

        lax.fori_loop(0, HALO // 8, body, 0)

    @pl.when(band == 0)
    def _():
        blank(0)

    @pl.when(band == bands - 1)
    def _():
        blank(low)

    def edge(lo, hi):
        for buf in (raised, flux):
            for c in range(wins):
                buf[c, pl.ds(8 * lo, 8), :] = zero
                buf[c, pl.ds(8 * hi + 8, 8), :] = zero

    acc[...] = jnp.zeros_like(acc)
    pltpu.make_async_copy(table, rows_in, load_sem.at[5]).wait()

    @pl.when(down_ok)
    def _():
        st_above().wait_recv()

    @pl.when(up_ok)
    def _():
        st_below().wait_recv()

    def lon_diff(xs, c):
        lane = lax.broadcasted_iota(jnp.int32, xs[c].shape, 1)
        after, before = xs[(c + 1) % wins], xs[c - 1]
        east_of = pltpu.roll(jnp.where(lane == 0, after, xs[c]), 127, 1)
        return east_of - pltpu.roll(jnp.where(lane == 127, before, xs[c]), 1, 1)

    def lon_diffs(xs):
        return [lon_diff(xs, c) for c in range(wins)]

    def lat_diff(ref, c, r0, high):
        return ref[c, pl.ds(r0 + 9, high), :] - ref[c, pl.ds(r0 + 7, high), :]

    def sweep(lo, hi, body):
        n = -(-(hi - lo) // STRIPS)
        size, more = divmod(hi - lo, n)
        at = lo
        for length, times in ((size + 1, more), (size, n - more)):
            if times:
                def turns(i, _, at=at, length=length):
                    r0 = pl.multiple_of(8 * (at + i * length), 8)
                    body(r0, 8 * length, pl.ds(r0, 8 * length), pl.ds(pl.multiple_of(r0 + 8, 8), 8 * length))
                    return 0

                lax.fori_loop(0, times, turns, 0)
                at += length * times

    def strip_sum(xs):
        return jnp.sum(sum(xs).reshape(-1, 8, 128), axis=0)

    def run(kind, source, s, lo, hi, finish, target_of=None):
        def push(h, c, at, step):
            if kind != "forced":
                return 0.5 * h
            base = 2 * (s * STEPS + step)
            return 0.5 * (h + (trig[base] * st[2, c, at, :] + trig[base + 1] * st[3, c, at, :]))

        def begin(r0, high_rows, at, padded):
            for c in range(wins):
                raised[c, padded, :] = push(source[s, c, 0, at, :], c, at, 0)

        sweep(lo, hi, begin)
        edge(lo, hi)

        def advance(step, is_first, is_last):
            def first(r0, high_rows, at, padded):
                slopes = lon_diffs([raised[c, padded, :] for c in range(wins)])
                cor = rows_in[0, at, :]
                for c in range(wins):
                    wet, sea = st[0, c, at, :], st[1, c, at, :]
                    dx, dy = slopes[c], lat_diff(raised, c, r0, high_rows)
                    if is_first:
                        u, v = source[s, c, 1, at, :], source[s, c, 2, at, :]
                    else:
                        u, v = east[c, at, :], north[c, at, :]
                    if kind == "back":
                        e = sea * (u + wet * dx)
                        f = sea * (v + wet * dy)
                        east[c, at, :] = DRAG_RATE * e - cor * f
                        north[c, at, :] = cor * e + DRAG_RATE * f
                        fluy[c, at, :], flux[c, padded, :] = 0.5 * e, 0.5 * f
                    else:
                        e = sea * (DRAG_RATE * u + cor * v - dx)
                        f = sea * (DRAG_RATE * v - cor * u - dy)
                        half = 0.5 * wet
                        east[c, at, :], north[c, at, :] = e, f
                        fluy[c, at, :], flux[c, padded, :] = half * e, half * f

            sweep(lo, hi, first)

            def second(r0, high_rows, at, padded):
                slopes = lon_diffs([fluy[c, at, :] for c in range(wins)])
                inside = rows_in[1, at, :]
                sums = []
                for c in range(wins):
                    d = slopes[c] + lat_diff(flux, c, r0, high_rows)
                    h = source[s, c, 0, at, :] if is_first else high[c, at, :]
                    h = (h + d if kind == "back" else h - d) * inside
                    if not is_last:
                        high[c, at, :], raised[c, padded, :] = h, push(h, c, at, step + 1)
                        continue
                    values = finish(c, at, (h, east[c, at, :], north[c, at, :]))
                    if kind == "free":
                        if c < per:
                            sums.append(values)
                    else:
                        target, slot = target_of
                        for a in range(3):
                            target[slot, c, a, at, :] = values[a]
                if sums:
                    acc[0] += strip_sum([x for x, _ in sums])
                    acc[1] += strip_sum([x for _, x in sums])

            inner = 1 if is_last else 0
            sweep(lo + inner, hi - inner, second)

        advance(0, True, False)

        def middle(step, _):
            advance(step, False, False)
            return 0

        lax.fori_loop(1, STEPS - 1, middle, 0)
        advance(STEPS - 1, False, True)

    def keep(c, at, values):
        return values

    def arrive(n):
        s = turn(n)
        piece(s, s).wait_recv()
        send_halo(s)

    def subtract(s, first_strip, last_strip):
        after = lax.rem(s + 1, sections)
        at = pl.ds(8 * first_strip, 8 * (last_strip - first_strip))

        def body(c, _):
            for a in range(3):
                mis[s, c, a, at, :] = mis[s, c, a, at, :] - start[after, c, a, at, :]
            return 0

        lax.fori_loop(0, wins, body, 0)

    columns = pl.ds(me * per, per)

    def give(source, target, send, recv, s, at_columns, slot):
        return pltpu.make_async_remote_copy(
            src_ref=source.at[s, pl.ds(0, per), :, pl.ds(top, rows), :],
            dst_ref=target.at[at_columns],
            send_sem=send.at[s], recv_sem=recv.at[slot],
            device_id={"sec": s}, device_id_type=MESH,
        )

    def send_mismatch(n):
        subtract(turn(n), top // 8, low // 8)
        give(mis, home, s2, r2, turn(n), columns, me).start()

    even = lax.rem(me, 2) == 0

    def forced(n, _):
        @pl.when(n == 1)
        def _():
            for i in range(1, sections - 1):
                arrive(i)
            for i in range(1, sections - 1):
                piece(turn(i), me).wait_send()

        s = turn(n)
        recv_halo(s)
        run("forced", start, s, 0, strips, keep, (mis, s))

        late = jnp.logical_and(n == sections - 2, even)

        @pl.when(jnp.logical_and(n > 0, jnp.logical_not(late)))
        def _():
            send_mismatch(n)

        @pl.when(n == sections - 2)
        def _():
            arrive(sections - 1)

        @pl.when(late)
        def _():
            send_mismatch(n)

        return 0

    lax.fori_loop(0, sections, forced, 0)
    subtract(me, top // 8, low // 8)
    own_mis = pltpu.make_async_copy(
        mis.at[me, pl.ds(0, per), :, pl.ds(top, rows), :],
        home.at[columns],
        own_sem.at[1],
    )
    own_mis.start()

    def fringe(s, _):
        subtract(s, 1, top // 8)
        subtract(s, low // 8, strips - 1)
        return 0

    lax.fori_loop(0, sections, fringe, 0)

    def back(i, _):
        s = turn(lax.rem(jnp.where(i < sections, order(i), i), sections))
        before = lax.rem(s + sections - 1, sections)

        def done(c, at, values):
            return [x - mis[before, c, a, at, :] for a, x in enumerate(values)]

        run("back", mis, s, 1, strips - 1, done, (grad, s))

        @pl.when(i < sections)
        def _():
            give(grad, full, s3, r3, s, columns, me).start()

        return 0

    lax.fori_loop(1, sections + 1, back, 0)
    own_grad = pltpu.make_async_copy(
        grad.at[me, pl.ds(0, per), :, pl.ds(top, rows), :],
        full.at[columns],
        own_sem.at[2],
    )
    own_grad.start()

    def image(i, _):
        s = peer(i)
        after = peer(i + 1)

        def squares(c, at, values):
            pairs = [(x, grad[after, c, a, at, :]) for a, x in enumerate(values)]
            return sum(g * g for _, g in pairs), sum((x - g) * (x - g) for x, g in pairs)

        run("free", grad, s, 2, strips - 2, squares)
        return 0

    lax.fori_loop(0, sections, image, 0)

    total[band] = acc[...]

    def share_total(j, slot):
        return pltpu.make_async_remote_copy(
            src_ref=acc, dst_ref=total.at[slot], send_sem=ts.at[j], recv_sem=tr.at[slot],
            device_id={"lat": j}, device_id_type=MESH,
        )

    for i in range(1, bands):
        share_total(lax.rem(band + i, bands), band).start()
    for i in range(1, bands):
        j = lax.rem(band + i, bands)
        share_total(j, j).wait_recv()
    for i in range(1, bands):
        share_total(lax.rem(band + i, bands), band).wait_send()
    summed = total[0]
    for s in range(1, bands):
        summed = summed + total[s]
    acc[...] = summed
    part[me] = summed

    def share_part(j, slot):
        return pltpu.make_async_remote_copy(
            src_ref=acc, dst_ref=part.at[slot], send_sem=ps.at[j], recv_sem=pr.at[slot],
            device_id={"sec": j}, device_id_type=MESH,
        )

    for i in range(1, sections):
        share_part(peer(i), me).start()

    def rest(n, _):
        give(grad, full, s3, r3, turn(n), columns, me).start()
        return 0

    for i in range(1, sections):
        share_part(peer(i), peer(i)).wait_recv()
    summed = part[0]
    for s in range(1, sections):
        summed = summed + part[s]
    sums = jnp.sum(jnp.sum(summed, axis=2, keepdims=True), axis=1, keepdims=True)
    step = sums[0] / count / (sums[1] / count + EPSILON)
    step_out[...] = jnp.broadcast_to(step, (8, 128))

    own_mis.wait()

    def mismatches(i, _):
        s = peer(i)
        give(mis, home, s2, r2, s, columns, s).wait()
        return 0

    lax.fori_loop(1, sections, mismatches, 0)

    own_grad.wait()

    def grads(i, _):
        s = peer(i)
        give(grad, full, s3, r3, s, columns, s).wait_recv()
        return 0

    lax.fori_loop(1, sections, grads, 0)


    piece(turn(sections - 1), me).wait_send()

    def drain(i, _):
        s = peer(i)
        give(grad, full, s3, r3, s, columns, me).wait_send()
        return 0

    lax.fori_loop(1, sections, drain, 0)

    def drain_halo(i, _):
        s = peer(i)

        @pl.when(up_ok)
        def _():
            to_above(s).wait_send()

        @pl.when(down_ok)
        def _():
            to_below(s).wait_send()

        return 0

    lax.fori_loop(0, sections, drain_halo, 0)

    @pl.when(up_ok)
    def _():
        st_above().wait_send()

    @pl.when(down_ok)
    def _():
        st_below().wait_send()

    for i in range(1, sections):
        share_part(peer(i), me).wait_send()


def finish_kernel(fields, home, full, step, new_fields, mismatch, step_out):
    rows, width = fields.shape[1:]
    length = step[0:1, :]
    step_out[0, 0] = step[0, 0]

    def body(r, _):
        at = pl.ds(pl.multiple_of(8 * r, 8), 8)
        for c in range(width // 128):
            cols = slice(c * 128, c * 128 + 128)
            for a in range(3):
                new_fields[a, at, cols] = fields[a, at, cols] - length * full[c, a, at, :]
                mismatch[a, at, cols] = home[c, a, at, :]
        return 0

    lax.fori_loop(0, rows // 8, body, 0)


def shards(states, depth_field, land_mask, tide_cos, tide_sin):
    fields = states[0]
    rows, lon = fields.shape[1:]
    sections, bands = lax.axis_size("sec"), lax.axis_size("lat")
    share = lon // sections
    tall = rows + 2 * HALO
    lat_total = rows * bands
    ids = np.arange(lat_total + 2 * HALO, dtype=np.float32) - HALO
    inside = ((ids >= 0) & (ids < lat_total)).astype(np.float32)
    turned = np.float32(math.pi) * (ids + np.float32(0.5)) / np.float32(lat_total)
    coriolis = np.float32(CORIOLIS_MAX) * np.sin(turned - np.float32(0.5 * math.pi))
    row_table = np.broadcast_to(np.stack([coriolis, inside])[:, :, None], (2, ids.size, 128))
    row_table = jnp.asarray(row_table.astype(np.float32))
    angles = np.float32(TWO_PI) * np.arange(sections * STEPS, dtype=np.float32) / np.float32(
        sections * STEPS
    )
    trig = jnp.asarray(np.stack([np.cos(angles), np.sin(angles)], axis=1).reshape(-1))
    f32 = jnp.float32
    dma = pltpu.SemaphoreType.DMA
    any_spec = pl.BlockSpec(memory_space=pl.ANY)
    vmem = pl.BlockSpec(memory_space=pltpu.VMEM)
    tiles, wins = lon // 128, share // 128 + 1
    stacked = pltpu.VMEM((sections, wins, 3, tall, 128), f32)
    plain = pltpu.VMEM((wins, tall, 128), f32)
    padded = pltpu.VMEM((wins, tall + 16, 128), f32)
    gathered = jax.ShapeDtypeStruct((tiles, 3, rows, 128), f32)
    home, full, step = pl.pallas_call(
        functools.partial(kernel, sections, bands, float(sections * 3 * lat_total * lon)),
        out_shape=(
            gathered,
            gathered,
            jax.ShapeDtypeStruct((8, 128), f32),
        ),
        in_specs=[any_spec] * 6 + [pl.BlockSpec(memory_space=pltpu.SMEM)],
        out_specs=(any_spec, any_spec, vmem),
        scratch_shapes=[
            pltpu.VMEM((3, rows, lon), f32),
            pltpu.VMEM((3, rows, share + 256), f32),
            pltpu.VMEM((rows, share + 256), jnp.int32),
            pltpu.VMEM((2, tall, 128), f32),
            pltpu.VMEM((sections, wins, 3, rows, 128), f32),
            pltpu.VMEM((4, wins, tall, 128), f32),
            stacked, stacked, stacked,
            plain, plain, plain, padded, padded, plain,
            pltpu.VMEM((2, 8, 128), f32),
            pltpu.VMEM((sections, 2, 8, 128), f32),
            pltpu.VMEM((bands, 2, 8, 128), f32),
            dma((6,)),
            dma((sections,)), dma((sections,)),
            dma((2, sections)), dma((2, sections)),
            dma((2,)), dma((2,)),
            dma((sections,)), dma((sections,)),
            dma((sections,)), dma((sections,)),
            dma((3,)),
            dma((sections,)), dma((sections,)),
            dma((bands,)), dma((bands,)),
        ],
        compiler_params=pltpu.CompilerParams(
            collective_id=0, has_side_effects=True, vmem_limit_bytes=60 * 1024 * 1024
        ),
        name="shooting",
    )(fields, depth_field, land_mask, tide_cos, tide_sin, row_table, trig)
    half = 2 * share
    block = pl.BlockSpec((3, rows, half), lambda i: (0, 0, i))
    by_tile = pl.BlockSpec((half // 128, 3, rows, 128), lambda i: (i, 0, 0, 0))
    new_fields, mismatch, length = pl.pallas_call(
        finish_kernel,
        grid=(sections // 2,),
        out_shape=(jax.ShapeDtypeStruct(fields.shape, f32),) * 2 + (jax.ShapeDtypeStruct((1, 1), f32),),
        in_specs=[block, by_tile, by_tile, pl.BlockSpec((8, 128), lambda i: (0, 0))],
        out_specs=(block, block, pl.BlockSpec(memory_space=pltpu.SMEM)),
        compiler_params=pltpu.CompilerParams(vmem_limit_bytes=60 * 1024 * 1024),
        name="update",
    )(fields, home, full, step)
    return new_fields[None], mismatch[None], length.reshape(())


def solution(mesh):
    return jax.shard_map(
        shards,
        mesh=mesh,
        in_specs=(
            P("sec", None, "lat", None),
            P("lat", None),
            P("lat", None),
            P("lat", None),
            P("lat", None),
        ),
        out_specs=(P("sec", None, "lat", None), P("sec", None, "lat", None), P()),
        check_vma=False,
    )
```
